128 devices in a mesh: area: 4 (over y), dev: 32 (over z, x, core).
Axes of the slice: x: 4, y: 4, z: 4, core: 2. Of those that a mesh axis runs over, the one named last changes fastest.
Arguments:
- initial_state: float32 [3, 2097152], P(None, ('area', 'dev')), may hold values from -7 to 0.9, as said below
- waveform_guess: bfloat16 [10, 2097152], P(None, ('area', 'dev')), may hold values from -7 to -2
- drive_current: float32 [10, 2097152], P(None, ('area', 'dev')), may hold values from -6 to 6
- conductance: bfloat16 [8, 128, 128], replicated, may hold values from 0 to 0.31, as said below
- partners: int32 [16384, 4], P(('area', 'dev')), may hold values from 0 to 31, all different within a row; in each aligned block of 128 rows (0 to 127, 128 to 255, ...) at most 32 rows name the same one
- partner_slot: int32 [16384, 4], P(('area', 'dev')), may hold values from 0 to 127
- cond_index: int32 [16384, 5], P(('area', 'dev')), may hold values from 0 to 7
- remote_block: int32 [16384], P(('area', 'dev')), may hold values from 0 to 127
Outputs:
- voltage: float32 [10, 2097152], P(None, ('area', 'dev'))
- gating: float32 [2, 2097152], P(None, ('area', 'dev'))
The draws below stay inside these ranges and needn't reach their ends.
Inputs may be any that keep to these rules, and one draw needn't show every extreme that they name: `partners`: each row names 4 different devices; among the rows of one device at most 32 name the same device, and that many do on some device. `initial_state`: voltages in the first row, h in the second, n in the third. `conductance`: entries are non-negative.
All inputs are finite; a program needn't handle non-finite values.
Results may differ from the reference program's by a relative error of at most 0.0021.
Values may be sent and summed in bfloat16 or wider, within the bound.
A program may use at most 128 MiB of HBM per device.

```python
import math
import jax
import jax.numpy as jnp
import numpy as np
from jax import lax

NB = 128
BLK_DEV = 128
K = 10
ITERS = 2
NEWTON = 3
NP = 4
NCOND = 8
CAP = 32
BLOCKS = 16384
NEURONS = 2097152
N_AREA = 4
N_DEV = 32


def draw_initial_state(key, part):
    key = jax.random.fold_in(key, 11)
    key_volt, key_inact, key_act = jax.random.split(key, 3)
    spread_volt = jax.random.uniform(key_volt, (NEURONS,), jnp.float32)
    spread_inact = jax.random.uniform(key_inact, (NEURONS,), jnp.float32)
    spread_act = jax.random.uniform(key_act, (NEURONS,), jnp.float32)
    voltage = -7.0 + 5.0 * spread_volt
    inactive = 0.2 + 0.7 * spread_inact
    active = 0.1 + 0.5 * spread_act
    return jnp.stack([voltage, inactive, active]).astype(jnp.float32)


def draw_conductance(key, part):
    key = jax.random.fold_in(key, 23)
    key_off, key_diag = jax.random.split(key, 2)
    shape_all = (NCOND, NB, NB)
    row_ids = lax.broadcasted_iota(jnp.int32, shape_all, 1)
    col_ids = lax.broadcasted_iota(jnp.int32, shape_all, 2)
    offdiag = jax.random.uniform(key_off, shape_all, jnp.float32) * (0.4 / NB)
    diagonal = jnp.exp(jax.random.uniform(key_diag, shape_all, jnp.float32, minval=math.log(0.05), maxval=math.log(0.3)))
    return jnp.where(row_ids == col_ids, diagonal, offdiag).astype(jnp.bfloat16)


def set_ends(drawn, own_key, least, high):
    longest = drawn.shape.index(max(drawn.shape))
    spots = []
    for shift in (0, 1):
        where = [jax.random.randint(jax.random.fold_in(own_key, axis), (), 0, length) for axis, length in enumerate(drawn.shape)]
        where[longest] = (where[longest] + shift) % drawn.shape[longest]
        spots.append(tuple(where))
    return drawn.at[spots[0]].set(least).at[spots[1]].set(high)


def level_of(key, dims, cuts, low, largest):
    level, own = 1.0, jax.random.fold_in(key, 6)
    for axis_at, blocks in cuts:
        heights = jnp.exp(jax.random.uniform(jax.random.fold_in(own, axis_at), (blocks,), jnp.float32, low / len(cuts), largest / len(cuts)))
        level = level * jnp.repeat(heights, dims[axis_at] // blocks).reshape([-1 if axis == axis_at else 1 for axis in range(len(dims))])
    return level


def shared_out(rng, own, number, rows, amount, top, limit, skew):
    ranking = jax.random.permutation(rng, amount)
    heavy_load, usual = load_shares(amount, rows * top, limit, skew, True), load_shares(amount, rows * top, limit, skew, False)
    places = jnp.arange(amount)

    def named(sizes, turn):
        used = int((sizes > 0).sum())
        fixed = max(1, used // 4)
        passed = fixed + (places - fixed + turn * (used - fixed)) % max(1, amount - fixed)
        return jnp.zeros((amount,), jnp.int32).at[ranking[jnp.where(places < fixed, places, passed)]].set(jnp.asarray(sizes, jnp.int32))

    sizes = jnp.where(number % 4 == 0, named(heavy_load, number // 4), named(usual, number - number // 4 - 1))
    mixed = jax.random.permutation(jax.random.fold_in(own, 3), amount)
    source_of, sink = mixed[0:amount // 2 * 2:2], mixed[1:amount // 2 * 2:2]
    margin = jnp.minimum(sizes[source_of] - 1, limit - sizes[sink]) // 2
    margin = jnp.where((source_of == ranking[0]) | (sink == ranking[0]) | (sizes[sink] == 0), 0, jnp.maximum(margin, 0))
    passed = jax.random.randint(jax.random.fold_in(own, 4), (amount // 2,), 0, 1 << 20) % (margin + 1)
    sizes = sizes.at[source_of].add(-passed).at[sink].add(passed)
    members = jnp.searchsorted(jnp.cumsum(sizes), jnp.arange(rows * top), side="right").astype(jnp.int32)
    table = members.reshape(top, rows).T
    table = table[jax.random.permutation(jax.random.fold_in(own, 1), rows)]
    turn = jax.random.randint(jax.random.fold_in(own, 2), (rows, 1), 0, top)
    return jnp.take_along_axis(table, (jnp.arange(top)[None, :] + turn) % top, axis=1)


def load_shares(count, total, reach, slope, full):
    portions = [(1 << 20) // math.isqrt(grade ** slope) + 1 for grade in range(1, count + 1)]
    largest = reach if full else min(reach, max(-(-total // count), total * portions[0] // sum(portions)))
    least = 1 if total - largest >= count - 1 else 0
    counts, rest = [largest] + [least] * (count - 1), total - largest - least * (count - 1)
    while rest > 0:
        candidates = [i for i in range(1, count) if counts[i] < largest] or [i for i in range(1, count) if counts[i] < reach]
        pool, left = sum([portions[i] for i in candidates]), rest
        for i in candidates:
            more = min(reach - counts[i], max(1, left * portions[i] // pool), rest)
            counts[i] = counts[i] + more
            rest = rest - more
    return np.array(counts)


def gaussian(stream_key, shape, scale, reach, shards=(), kind=jnp.bfloat16):
    array = jax.random.normal(stream_key, shape, jnp.float32) * scale
    if len(shards) > 0:
        array = level_of(stream_key, shape, shards, -0.22, 0.18) * array
    return jnp.clip(array, min=-reach, max=reach).astype(kind)


def setup_inputs(seed: int = 0) -> dict:
    key_of = jax.random.split(jax.random.key(seed), 9)
    initial_state = draw_initial_state(jax.random.fold_in(key_of[8], 71), 0)
    waveform_guess = jnp.clip(-7.0 + 5.0 * jax.random.uniform(key_of[1], (K, NEURONS), jnp.float32) ** level_of(key_of[1], (K, NEURONS), ((1, 128),), -0.2, 0.2), -7.0, -2.0).astype(jnp.bfloat16)
    drive_current = gaussian(key_of[2], (K, NEURONS), 1.0, 6.0, ((1, 128),), jnp.float32)
    conductance = draw_conductance(jax.random.fold_in(key_of[8], 71), 0)
    partners_keys = jax.random.split(jax.random.fold_in(key_of[4], 1), BLOCKS // BLK_DEV)
    partners_turns = jax.random.permutation(jax.random.fold_in(key_of[4], 3), BLOCKS // BLK_DEV)
    partners = jax.vmap(lambda own, number: shared_out(jax.random.fold_in(key_of[4], 2), own, number, BLK_DEV, N_DEV, NP, CAP, 2))(partners_keys, partners_turns).reshape((BLOCKS, NP))
    partner_slot = set_ends(jax.random.randint(key_of[5], (BLOCKS, NP), 0, BLK_DEV), jax.random.fold_in(key_of[5], 1), 0, BLK_DEV - 1).astype(jnp.int32)
    cond_index = set_ends(jax.random.randint(key_of[6], (BLOCKS, NP + 1), 0, NCOND), jax.random.fold_in(key_of[6], 1), 0, NCOND - 1).astype(jnp.int32)
    remote_block = set_ends(jax.random.randint(key_of[7], (BLOCKS,), 0, BLK_DEV), jax.random.fold_in(key_of[7], 1), 0, BLK_DEV - 1).astype(jnp.int32)
    return {"initial_state": initial_state, "waveform_guess": waveform_guess, "drive_current": drive_current, "conductance": conductance, "partners": partners, "partner_slot": partner_slot, "cond_index": cond_index, "remote_block": remote_block}


time_step = 0.05
g_sodium = 35.0
g_potassium = 9.0
g_leakage = 0.1
e_sodium = 5.5
e_potassium = -9.0
e_leakage = -6.5


def relax_gate(value, target, tau):
    return target + (value - target) * jnp.exp(-time_step / tau)


def integrate(initial_state, drive_current, inflow, leakage):
    voltage = initial_state[0]
    inactive = initial_state[1]
    active = initial_state[2]
    history = []
    for number in range(K):
        h_target = jax.nn.sigmoid(-(voltage + 5.8) / 0.7)
        h_tau = 0.6 + 3.0 / jnp.cosh((voltage + 5.8) / 1.4)
        inactive = relax_gate(inactive, h_target, h_tau)
        n_target = jax.nn.sigmoid(voltage + 3.0)
        n_tau = 0.5 + 4.0 / jnp.cosh((voltage + 3.0) / 2.0)
        active = relax_gate(active, n_target, n_tau)
        previous = voltage
        fourth = active ** 4
        for newton in range(NEWTON):
            opening = jax.nn.sigmoid((voltage + 3.5) / 0.8)
            slope_m = opening * (1.0 - opening) / 0.8
            residual = ((voltage - previous) / time_step
                        + g_sodium * opening ** 3 * inactive * (voltage - e_sodium)
                        + g_potassium * fourth * (voltage - e_potassium)
                        + g_leakage * (voltage - e_leakage)
                        + leakage * voltage - inflow[number] - drive_current[number])
            jacobian = (1.0 / time_step
                        + g_sodium * inactive * (3.0 * opening ** 2 * slope_m * (voltage - e_sodium) + opening ** 3)
                        + g_potassium * fourth + g_leakage + leakage)
            jacobian = jnp.maximum(jacobian, 0.5 / time_step)
            voltage = voltage - residual / jacobian
        history.append(voltage)
    return jnp.stack(history), jnp.stack([inactive, active])


def couple(waveform, float_conductance, targets, cond_index):
    blocked = waveform.reshape(K, BLOCKS, NB).transpose(1, 0, 2)

    def accumulate(carry, portion):
        start_row = portion * BLK_DEV
        pieces = lax.dynamic_slice_in_dim(blocked, start_row, BLK_DEV, 0).astype(jnp.float32)
        kinds = lax.dynamic_slice_in_dim(cond_index, start_row, BLK_DEV, 0)
        places = lax.dynamic_slice_in_dim(targets, start_row, BLK_DEV, 0)
        chosen = float_conductance[kinds]
        message = jnp.einsum('bkn,bpnm->bpkm', pieces, chosen, precision=lax.Precision.HIGHEST)
        carry = carry.at[places.reshape(-1)].add(message.reshape(-1, K, NB))
        return carry, None

    initial = jnp.zeros((BLOCKS, K, NB), jnp.float32)
    summed, unused = lax.scan(accumulate, initial, jnp.arange(BLOCKS // BLK_DEV, dtype=jnp.int32))
    return summed.transpose(1, 0, 2).reshape(K, NEURONS)


def reference(initial_state, waveform_guess, drive_current, conductance, partners, partner_slot, cond_index, remote_block):
    block_ids = jnp.arange(BLOCKS, dtype=jnp.int32)
    area_of = block_ids // (N_DEV * BLK_DEV)
    dev_of = (block_ids // BLK_DEV) % N_DEV
    inner_targets = (area_of[:, None] * N_DEV + partners) * BLK_DEV + partner_slot
    outer_targets = ((((area_of + 1) % N_AREA) * N_DEV + dev_of) * BLK_DEV + remote_block)[:, None]
    targets = jnp.concatenate([inner_targets, outer_targets], axis=1).astype(jnp.int32)
    float_conductance = conductance.astype(jnp.float32)
    column_sums = jnp.sum(float_conductance, axis=1)
    leak_blocks = jnp.zeros((BLOCKS, NB), jnp.float32).at[targets.reshape(-1)].add(column_sums[cond_index.reshape(-1)])
    leakage = leak_blocks.reshape(NEURONS)
    waveform = waveform_guess
    voltage = None
    gating = None
    for iteration in range(ITERS):
        inflow = couple(waveform, float_conductance, targets, cond_index)
        voltage, gating = integrate(initial_state, drive_current, inflow, leakage)
        waveform = voltage.astype(jnp.bfloat16)
    return voltage, gating
```

```python
import functools

import jax
import jax.numpy as jnp
from jax import lax
from jax.experimental import pallas as pl
from jax.experimental.pallas import tpu as pltpu
from jax.sharding import PartitionSpec as P

MESH = pl.DeviceIdType.MESH
K = 10
ITERS = 2
NEWTON = 3
CHUNKS = K * ITERS
NB = 128
CAP = 32
KINDS = 8
AHEAD_GATHER = 4
AHEAD_SELECT = 2
LOG2E = 1.4426950408889634
BF = jnp.bfloat16
F32 = jnp.float32
I32 = jnp.int32


def place():
    area = lax.axis_index("area")
    dev = lax.axis_index("dev")
    core = dev % 2
    z = dev // 8
    x = (dev // 2) % 4
    first = z * (1 - core) + x * core
    second = x * (1 - core) + z * core
    first_unit = 8 * (1 - core) + 2 * core
    second_unit = 2 * (1 - core) + 8 * core
    return area, core, first, second, first_unit, second_unit


def device_at(by_area=0, by_first=0, by_second=0, by_core=0):
    area, core, first, second, first_unit, second_unit = place()
    dev = (
        ((first + by_first) % 4) * first_unit
        + ((second + by_second) % 4) * second_unit
        + (core + by_core) % 2
    )
    return ((area + by_area) % 4, dev)


def rcp(value):
    return pl.reciprocal(value, approx=True)


def gate_pair(shifted, scale):
    u = jnp.exp2(jnp.minimum(shifted * (LOG2E * scale), 20.0 * LOG2E))
    return u, 1.0 + u * u


def step_neurons(v, h, n, leak, drive_in):
    u, bottom = gate_pair(v + 5.8, 1.0 / 1.4)
    target = rcp(bottom)
    tau = 0.6 + 6.0 * (u * target)
    h = target + (h - target) * jnp.exp2((-0.05 * LOG2E) * rcp(tau))
    u, bottom = gate_pair(v + 3.0, -0.5)
    target = rcp(bottom)
    tau = 0.5 + 8.0 * (u * target)
    n = target + (n - target) * jnp.exp2((-0.05 * LOG2E) * rcp(tau))
    square = n * n
    potassium = 9.0 * (square * square)
    linear = leak + potassium + 20.1
    offset = 20.0 * v - 9.0 * potassium - 0.65 + drive_in
    sodium = 35.0 * h
    for _ in range(NEWTON):
        m = rcp(1.0 + jnp.exp2(v * (-1.25 * LOG2E) - 3.5 * 1.25 * LOG2E))
        q = sodium * (m * m * m)
        w = v - 5.5
        residual = linear * v - offset + q * w
        jacobian = linear + q * (1.0 + (3.75 * w) * (1.0 - m))
        v = v - residual * rcp(jnp.maximum(jacobian, 10.0))
    return v, h, n


def kernel(
    wave0, drive, state, cond, lists, volt, gate,
    ag, picked, rcv, select, group, now, leak, m1s, m1r, m2s, m2r,
    send1, recv1, send2, recv2, sendy, recvy, sendm1, recvm1, sendm2, recvm2,
):
    area, core, first, second, first_unit, second_unit = place()
    barrier = pltpu.get_barrier_semaphore()
    greet = [device_at(by_first=o, by_core=c) for o in (1, 2, 3) for c in (0, 1)]
    greet += [device_at(by_second=o, by_core=c) for o in (1, 2, 3) for c in (0, 1)]
    greet += [device_at(by_core=1), device_at(by_area=1), device_at(by_area=3)]
    for other in greet:
        pl.semaphore_signal(barrier, inc=1, device_id=other, device_id_type=MESH)

    for k in range(K):
        ag[k, 0] = wave0[k]
    rows = lax.broadcasted_iota(I32, (32, NB), 0)
    target = (
        ((first + (rows >> 3)) & 3) * first_unit
        + ((second + ((rows >> 1) & 3)) & 3) * second_unit
        + ((core + rows) & 1)
    )
    hit = jnp.zeros((32, NB), F32)
    slot = jnp.zeros((32, NB), I32)
    kind = jnp.zeros((32, NB), I32)
    for p in range(4):
        same = lists[p : p + 1, :] == target
        hit = jnp.where(same, 1.0, hit)
        slot = jnp.where(same, lists[4 + p : 5 + p, :], slot)
        kind = jnp.where(same, lists[8 + p : 9 + p, :], kind)
    before = lax.broadcasted_iota(I32, (NB, NB), 0) < lax.broadcasted_iota(I32, (NB, NB), 1)
    rank = jnp.dot(hit.astype(BF), jnp.where(before, 1.0, 0.0).astype(BF), preferred_element_type=F32)
    rank = jnp.where(hit > 0.5, rank, -1.0).astype(I32)
    for o in range(4):
        part = slice(8 * o, 8 * o + 8)
        put = m1r.at[0] if o == 0 else m1s.at[o]
        put[0] = rank[part]
        put[1] = slot[part]
        put[2] = kind[part]
    m2s[0, 0] = jnp.broadcast_to(lists[13:14, :] + 1, (8, NB))
    m2s[0, 1] = jnp.broadcast_to(lists[12:13, :], (8, NB))

    pl.semaphore_wait(barrier, len(greet))

    def remote(src, dst, send, recv, **where):
        return pltpu.make_async_remote_copy(
            src_ref=src, dst_ref=dst, send_sem=send, recv_sem=recv,
            device_id=device_at(**where), device_id_type=MESH,
        )

    def gather(s):
        for o in (1, 3, 2):
            remote(ag.at[s, 0], ag.at[s, o], send1.at[s], recv1.at[s], by_first=o).start()
        remote(ag.at[s, 0], rcv.at[s, pl.ds(8 * NB, NB)], sendy.at[s], recvy.at[s], by_area=1).start()

    def spread(s):
        for j in (2, 3, 6, 7, 4, 5, 1):
            remote(
                picked.at[s, j - 1], rcv.at[s, pl.ds(j * NB, NB)], send2.at[s], recv2.at[s],
                by_second=j // 2, by_core=j % 2,
            ).start()

    def all_gathered(s):
        return remote(ag.at[s, pl.ds(1, 3)], ag.at[s, pl.ds(1, 3)], send1.at[s], recv1.at[s], by_first=1)

    def all_spread(s):
        return remote(picked.at[s], rcv.at[s, pl.ds(NB, 7 * NB)], send2.at[s], recv2.at[s], by_core=1)

    def all_far(s):
        return remote(ag.at[s, 0], rcv.at[s, pl.ds(8 * NB, NB)], sendy.at[s], recvy.at[s], by_area=1)

    for o in (1, 2, 3):
        remote(m1s.at[o], m1r.at[o], sendm1.at[o], recvm1.at[o], by_first=o).start()
    gather(0)
    remote(m2s.at[0], m2r.at[8], sendm2.at[0], recvm2.at[0], by_area=1).start()
    for s in range(1, AHEAD_GATHER):
        gather(s)
    for o in (1, 2, 3):
        remote(m1s.at[o], m1r.at[o], sendm1.at[o], recvm1.at[o], by_first=o).wait()

    spot = lax.broadcasted_iota(I32, (CAP, NB), 0)
    for o in range(4):
        for j in range(8):
            chosen = m1r[o, 0, j : j + 1, :] == spot
            select[o, j * CAP : (j + 1) * CAP, :] = jnp.where(chosen, 1.0, 0.0).astype(BF)

    def pick(s):
        all_gathered(s).wait_recv()
        for o in range(4):
            got = jnp.dot(select[o], ag[s, o], preferred_element_type=F32).astype(BF)
            part = pl.ds(o * CAP, CAP)
            rcv[s, part, :] = got[:CAP]
            for j in range(1, 8):
                picked[s, j - 1, part, :] = got[j * CAP : (j + 1) * CAP]
        spread(s)

    for s in range(AHEAD_SELECT):
        pick(s)
        gather(AHEAD_GATHER + s)

    meta = jnp.zeros((16, NB), F32)
    diagonal = (lax.broadcasted_iota(I32, (16, 256), 0) & 7) == (lax.broadcasted_iota(I32, (16, 256), 1) >> 5)
    for o in range(4):
        valid = m1r[o, 0] >= 0
        codes = jnp.concatenate(
            [jnp.where(valid, m1r[o, 1] + 1, 0), jnp.where(valid, m1r[o, 2], 0)], axis=0
        ).astype(F32).astype(BF)
        crossed = lax.dot_general(
            codes, select[o], (((1,), (1,)), ((), ())), preferred_element_type=F32
        )
        crossed = jnp.where(diagonal, crossed, 0.0).astype(BF)
        fold = (lax.broadcasted_iota(I32, (256, NB), 0) & 31) + 32 * o == lax.broadcasted_iota(I32, (256, NB), 1)
        meta = meta + jnp.dot(crossed, jnp.where(fold, 1.0, 0.0).astype(BF), preferred_element_type=F32)
    meta = meta.astype(I32)
    for j in range(8):
        put = m2r.at[0] if j == 0 else m2s.at[j]
        put[0] = jnp.broadcast_to(meta[j : j + 1, :], (8, NB))
        put[1] = jnp.broadcast_to(meta[8 + j : 9 + j, :], (8, NB))

    def send_meta(j):
        return remote(
            m2s.at[j], m2r.at[j], sendm2.at[j], recvm2.at[j], by_second=j // 2, by_core=j % 2
        )

    for j in range(1, 8):
        send_meta(j).start()
    for j in range(1, 8):
        send_meta(j).wait()
    remote(m2s.at[0], m2r.at[8], sendm2.at[0], recvm2.at[0], by_area=1).wait()

    cell = lax.broadcasted_iota(I32, (KINDS * NB, NB), 0)
    for j in range(9):
        place1 = m2r[j, 0, 0:1, :]
        code = jnp.where(place1 > 0, m2r[j, 1, 0:1, :] * NB + place1 - 1, -1)
        group[:, j * NB : (j + 1) * NB] = jnp.where(cell == code, 1.0, 0.0).astype(BF)
    counts = jnp.dot(group[...], jnp.ones((9 * NB, NB), BF), preferred_element_type=F32)
    total = jnp.zeros((NB, NB), F32)
    for c in range(KINDS):
        column = jnp.sum(cond[c].astype(F32), axis=0, keepdims=True)
        total = total + counts[c * NB : (c + 1) * NB] * column
    leak[...] = total

    def chunk(s, carry):
        k = s % K

        @pl.when(s + AHEAD_SELECT < CHUNKS)
        def _():
            pick(s + AHEAD_SELECT)

        @pl.when(s + AHEAD_SELECT + AHEAD_GATHER < CHUNKS)
        def _():
            gather(s + AHEAD_SELECT + AHEAD_GATHER)

        @pl.when(k == 0)
        def _():
            now[...] = state[...]

        all_spread(s).wait_recv()
        all_far(s).wait_recv()
        grouped = jnp.dot(group[...], rcv[s], preferred_element_type=F32)
        high = grouped.astype(BF)
        low = (grouped - high.astype(F32)).astype(BF)
        high = jnp.concatenate([high[c * NB : (c + 1) * NB] for c in range(KINDS)], axis=1)
        low = jnp.concatenate([low[c * NB : (c + 1) * NB] for c in range(KINDS)], axis=1)
        table = cond[...].reshape(KINDS * NB, NB)
        inflow = jnp.dot(high, table, preferred_element_type=F32) + jnp.dot(
            low, table, preferred_element_type=F32
        )
        part_rows = 64
        for g in range(NB // part_rows):
            part = slice(g * part_rows, (g + 1) * part_rows)
            v, h, n = step_neurons(
                now[0, part], now[1, part], now[2, part], leak[part], inflow[part] + drive[k, part]
            )
            now[0, part] = v
            now[1, part] = h
            now[2, part] = n
            volt[k, part] = v

        @pl.when(s < K)
        def _():
            ag[s + K, 0] = now[0].astype(BF)

        return carry

    lax.fori_loop(0, CHUNKS, chunk, 0)
    gate[...] = now[1:3]

    def drain(s, carry):
        all_gathered(s).wait_send()
        all_spread(s).wait_send()
        all_far(s).wait_send()
        return carry

    lax.fori_loop(0, CHUNKS, drain, 0)


def local(
    initial_state, waveform_guess, drive_current, conductance, partners, partner_slot, cond_index, remote_block
):
    wave0 = waveform_guess.reshape(K, NB, NB)
    drive = drive_current.reshape(K, NB, NB)
    state = initial_state.reshape(3, NB, NB)
    lists = jnp.concatenate(
        [partners.T, partner_slot.T, cond_index.T, remote_block[None, :], jnp.zeros((2, NB), I32)], axis=0
    )
    dma = pltpu.SemaphoreType.DMA
    volt, gate = pl.pallas_call(
        kernel,
        out_shape=(jax.ShapeDtypeStruct((K, NB, NB), F32), jax.ShapeDtypeStruct((2, NB, NB), F32)),
        in_specs=[pl.BlockSpec(memory_space=pltpu.VMEM)] * 5,
        out_specs=(pl.BlockSpec(memory_space=pltpu.VMEM),) * 2,
        scratch_shapes=[
            pltpu.VMEM((CHUNKS, 4, NB, NB), BF),
            pltpu.VMEM((CHUNKS, 7, NB, NB), BF),
            pltpu.VMEM((CHUNKS, 9 * NB, NB), BF),
            pltpu.VMEM((4, 8 * CAP, NB), BF),
            pltpu.VMEM((KINDS * NB, 9 * NB), BF),
            pltpu.VMEM((3, NB, NB), F32),
            pltpu.VMEM((NB, NB), F32),
            pltpu.VMEM((4, 3, 8, NB), I32),
            pltpu.VMEM((4, 3, 8, NB), I32),
            pltpu.VMEM((8, 2, 8, NB), I32),
            pltpu.VMEM((9, 2, 8, NB), I32),
            dma((CHUNKS,)), dma((CHUNKS,)), dma((CHUNKS,)), dma((CHUNKS,)), dma((CHUNKS,)), dma((CHUNKS,)),
            dma((4,)), dma((4,)), dma((8,)), dma((8,)),
        ],
        compiler_params=pltpu.CompilerParams(
            collective_id=0, has_side_effects=True, vmem_limit_bytes=48 * 1024 * 1024
        ),
        name="relax",
    )(wave0, drive, state, conductance, lists)
    return volt.reshape(K, NB * NB), gate.reshape(2, NB * NB)


def solution(mesh):
    in_specs = (
        P(None, ("area", "dev")),
        P(None, ("area", "dev")),
        P(None, ("area", "dev")),
        P(),
        P(("area", "dev"), None),
        P(("area", "dev"), None),
        P(("area", "dev"), None),
        P(("area", "dev")),
    )
    out_specs = (P(None, ("area", "dev")), P(None, ("area", "dev")))
    return jax.shard_map(local, mesh=mesh, in_specs=in_specs, out_specs=out_specs, check_vma=False)
```

```python
import functools

import jax
import jax.numpy as jnp
from jax import lax
from jax.experimental import pallas as pl
from jax.experimental.pallas import tpu as pltpu
from jax.sharding import PartitionSpec as P

MESH = pl.DeviceIdType.MESH
K = 10
ITERS = 2
NEWTON = 3
CHUNKS = K * ITERS
NB = 128
CAP = 32
KINDS = 8
AHEAD_GATHER = 8
AHEAD_RELAY = 5
AHEAD_SUM = 3
STEPS = 2380.0
MIDDLE = 2.0 * STEPS
EDGE = 10.0 * STEPS
COARSE = 32.0
LOG2E = 1.4426950408889634
BF = jnp.bfloat16
F32 = jnp.float32
I32 = jnp.int32


def rcp(value):
    return pl.reciprocal(value, approx=True)


def gate_pair(shifted, scale):
    u = jnp.exp2(jnp.minimum(shifted * (LOG2E * scale), 20.0 * LOG2E))
    return u, 1.0 + u * u


def step_neurons(v, h, n, leak, drive_in):
    u, bottom = gate_pair(v + 5.8, 1.0 / 1.4)
    target = rcp(bottom)
    tau = 0.6 + 6.0 * (u * target)
    h = target + (h - target) * jnp.exp2((-0.05 * LOG2E) * rcp(tau))
    u, bottom = gate_pair(v + 3.0, -0.5)
    target = rcp(bottom)
    tau = 0.5 + 8.0 * (u * target)
    n = target + (n - target) * jnp.exp2((-0.05 * LOG2E) * rcp(tau))
    square = n * n
    potassium = 9.0 * (square * square)
    linear = leak + potassium + 20.1
    offset = 20.0 * v - 9.0 * potassium - 0.65 + drive_in
    sodium = 35.0 * h
    for _ in range(NEWTON):
        m = rcp(1.0 + jnp.exp2(v * (-1.25 * LOG2E) - 3.5 * 1.25 * LOG2E))
        q = sodium * (m * m * m)
        w = v - 5.5
        residual = linear * v - offset + q * w
        jacobian = linear + q * (1.0 + (3.75 * w) * (1.0 - m))
        v = v - residual * rcp(jnp.maximum(jacobian, 10.0))
    return v, h, n


def dot(a, b, precision=None):
    return jnp.dot(a, b, preferred_element_type=F32, precision=precision)


def dot_last(a, b):
    return lax.dot_general(a, b, (((1,), (1,)), ((), ())), preferred_element_type=F32)


def kernel(
    wave0, drive, state, cond, lists, volt, gate,
    ag, far, sums_out, sums_in, own, select, masks, odd, place, tables, now, leak, enc, dec, left, m1s, m1r, mys, myr, m2s, m2r,
    send1, recv1, sendr, recvr, recvy, send2, recv2, sendm1, recvm1, sendmy, recvmy, sendm2, recvm2,
):
    dev = lax.axis_index("dev")
    core, x, z = dev % 2, (dev // 2) % 4, dev // 8
    area = lax.axis_index("area")
    over_z = [((z + o) % 4) * 8 + x * 2 for o in range(4)]
    column = [(area, over_z[o] + (core + c) % 2) for c in (0, 1) for o in range(4)]
    along = [(area, z * 8 + ((x + o) % 4) * 2 + core) for o in range(4)]
    sibling = column[4]
    next_area = ((area + 1) % 4, dev)
    barrier = pltpu.get_barrier_semaphore()
    greet = column[1:] + along[1:] + [next_area, ((area + 3) % 4, dev)]
    for other in greet:
        pl.semaphore_signal(barrier, inc=1, device_id=other, device_id_type=MESH)

    for k in range(K):
        ag[k, 0] = wave0[k]
    rows = lax.broadcasted_iota(I32, (32, NB), 0)
    target = ((z + (rows >> 3)) & 3) * 8 + ((x + rows) & 3) * 2 + ((core + (rows >> 2)) & 1)
    hit = jnp.zeros((32, NB), F32)
    slot = jnp.zeros((32, NB), I32)
    kind = jnp.zeros((32, NB), I32)
    for p in range(4):
        same = lists[p : p + 1, :] == target
        hit = jnp.where(same, 1.0, hit)
        slot = jnp.where(same, lists[4 + p : 5 + p, :], slot)
        kind = jnp.where(same, lists[8 + p : 9 + p, :], kind)
    lane = lax.broadcasted_iota(I32, (NB, NB), 1)
    line = lax.broadcasted_iota(I32, (NB, NB), 0)
    rank = dot(hit.astype(BF), jnp.where(line < lane, 1.0, 0.0).astype(BF))
    rank = jnp.where(hit > 0.5, rank, -1.0).astype(I32)
    for o in range(4):
        part = slice(8 * o, 8 * o + 8)
        put = m1r.at[0] if o == 0 else m1s.at[o]
        put[0] = rank[part]
        put[1] = slot[part]
        put[2] = kind[part]
    m1s[0] = m1r[0]
    mys[...] = lists[8:16, :]

    pl.semaphore_wait(barrier, len(greet))

    def remote(src, dst, send, recv, where):
        return pltpu.make_async_remote_copy(
            src_ref=src, dst_ref=dst, send_sem=send, recv_sem=recv,
            device_id=where, device_id_type=MESH,
        )

    def gather(s):
        mine = ag.at[s, 0]
        for o in (1, 3, 2):
            remote(mine, ag.at[s, o], send1.at[s], recv1.at[s], column[o]).start()
        remote(mine, ag.at[s, 4], send1.at[s], recvr.at[s], sibling).start()
        remote(mine, far.at[s], send1.at[s], recvy.at[s], next_area).start()

    def relay_copy(s):
        return remote(ag.at[s, pl.ds(1, 3)], ag.at[s, pl.ds(5, 3)], sendr.at[s], recvr.at[s], sibling)

    def relay(s):
        all_gathered(s).wait_recv()
        relay_copy(s).start()

    def spread(s):
        for o in (1, 3, 2):
            remote(sums_out.at[s, o - 1], sums_in.at[s, o - 1], send2.at[s], recv2.at[s], along[o]).start()

    def all_gathered(s):
        return remote(ag.at[s, pl.ds(1, 3)], ag.at[s, pl.ds(1, 3)], send1.at[s], recv1.at[s], column[1])

    def all_sent(s):
        return remote(ag.at[s, pl.ds(0, 5)], ag.at[s, pl.ds(0, 5)], send1.at[s], recv1.at[s], column[1])

    def all_relayed(s):
        return remote(ag.at[s, pl.ds(4, 4)], ag.at[s, pl.ds(4, 4)], sendr.at[s], recvr.at[s], sibling)

    def far_copy(s):
        return remote(ag.at[s, 0], far.at[s], send1.at[s], recvy.at[s], next_area)

    def all_spread(s):
        return remote(sums_out.at[s], sums_in.at[s], send2.at[s], recv2.at[s], along[1])

    def list_copy(b):
        return remote(m1s.at[b % 4], m1r.at[b], sendm1.at[b], recvm1.at[b], column[b])

    far_lists = remote(mys, myr, sendmy, recvmy, next_area)
    for b in range(1, 8):
        list_copy(b).start()
    far_lists.start()
    for s in range(AHEAD_GATHER):
        gather(s)
    for b in range(1, 8):
        list_copy(b).wait()
    far_lists.wait()

    spot = lax.broadcasted_iota(I32, (CAP, NB), 0)
    ones = jnp.ones((NB, NB), BF)
    blocks = [[] for _ in range(4)]
    kinds = [[] for _ in range(4)]
    for b in range(8):
        for d in range(4):
            row = (b // 4) * 4 + d
            chosen = m1r[b, 0, row : row + 1, :] == spot
            select[b, d * CAP : (d + 1) * CAP, :] = jnp.where(chosen, 1.0, 0.0).astype(BF)
            blocks[d].append(jnp.where(chosen, m1r[b, 1, row : row + 1, :] + 1, 0).astype(F32))
            kinds[d].append(jnp.where(chosen, m1r[b, 2, row : row + 1, :], 0).astype(F32))
    for s in range(AHEAD_RELAY):
        relay(s)
    links = []
    for d in range(4):
        for half in (0, 1):
            pieces = slice(4 * half, 4 * half + 4)
            links.append((
                jnp.concatenate(blocks[d][pieces], axis=0).astype(BF), jnp.concatenate(kinds[d][pieces], axis=0).astype(BF)
            ))
    links.append((
        jnp.where(line == lane, myr[5:6, :] + 1, 0).astype(F32).astype(BF),
        jnp.where(line == lane, myr[4:5, :], 0).astype(F32).astype(BF),
    ))
    for c in range(KINDS):
        tables[(c // 2) * NB : (c // 2 + 1) * NB, (c % 2) * NB : (c % 2 + 1) * NB] = cond[c]
    column_sums = [jnp.sum(cond[c].astype(F32), axis=0, keepdims=True) for c in range(KINDS)]
    column_sums = jnp.concatenate(column_sums + [jnp.zeros((NB - KINDS, NB), F32)], axis=0)
    eye = jnp.where(line == lane, 1.0, 0.0).astype(BF)
    counts = []
    for i, (block, table) in enumerate(links):
        part = slice(i * NB, (i + 1) * NB)
        block = dot(block, ones).astype(I32)
        table = dot(table, ones).astype(I32)
        for g in range(4):
            masks[g, part, :] = jnp.where((table >> 1) == g, 1.0, 0.0).astype(BF)
        odd[part, :] = table & 1
        to_block = dot_last(eye, jnp.where(block == lane + 1, 1.0, 0.0).astype(BF)).astype(BF)
        place[:, part] = to_block
        of_kind = jnp.where((table == lane) & (block > 0), 1.0, 0.0).astype(BF)
        counts.append(dot(to_block, of_kind))
    exact = lax.Precision.HIGHEST
    for d in (1, 2, 3):
        count = counts[2 * d] + counts[2 * d + 1]
        m2s[d - 1] = jnp.transpose(count)[0:8, :]
        remote(m2s.at[d - 1], m2r.at[d - 1], sendm2.at[d - 1], recvm2.at[d - 1], along[d]).start()
        bound = dot(count, column_sums, exact)
        enc[d - 1] = jnp.where(bound > 1e-30, STEPS / bound, 0.0)
    left[...] = jnp.zeros((3, NB, NB), F32)
    leak[...] = dot(counts[0] + counts[1] + counts[8], column_sums, exact)

    def add_up(s):
        all_relayed(s).wait_recv()
        far_copy(s).wait_recv()
        picked = [dot(select[b], ag[s, b]).astype(BF) for b in range(8)]
        waves = [got[d * CAP : (d + 1) * CAP] for d in range(4) for got in picked]
        waves = jnp.concatenate(waves + [far[s]], axis=0)
        both = dot(jnp.concatenate([waves * masks[g] for g in range(4)], axis=1), tables[...])
        message = jnp.where(odd[...] > 0, both[:, NB:], both[:, :NB])
        high = message.astype(BF)
        message = jnp.concatenate([high, (message - high.astype(F32)).astype(BF)], axis=1)
        for d in (1, 3, 2, 0):
            part = slice(2 * d * NB, 2 * (d + 1) * NB)
            total = dot(place[:, part], message[part])
            if d == 0:
                total = total + dot(place[:, 8 * NB :], message[8 * NB :])
            total = total[:, :NB] + total[:, NB:]
            if d == 0:
                own[s] = total
            else:
                code = total * enc[d - 1] + (left[d - 1] + MIDDLE)
                inner = jnp.clip(code, -EDGE, EDGE)
                code = jnp.clip(inner + (code - inner) * (1.0 / COARSE), -32767.0, 32767.0)
                sent = jnp.round(code)
                left[d - 1] = code - sent
                sums_out[s, d - 1] = sent.astype(I32).astype(jnp.int16)
        spread(s)

    for s in range(AHEAD_SUM):
        add_up(s)

    for d in (1, 2, 3):
        remote(m2s.at[d - 1], m2r.at[d - 1], sendm2.at[d - 1], recvm2.at[d - 1], along[d]).wait()
        count = jnp.transpose(jnp.concatenate([m2r[d - 1], jnp.zeros((NB - 8, NB), F32)], axis=0))
        bound = dot(count, column_sums, exact)
        dec[d - 1] = bound * (1.0 / STEPS)
        leak[...] += bound

    def chunk(s, carry):
        k = s % K

        @pl.when(s + AHEAD_GATHER < CHUNKS)
        def _():
            gather(s + AHEAD_GATHER)

        @pl.when(s + AHEAD_RELAY < CHUNKS)
        def _():
            relay(s + AHEAD_RELAY)

        @pl.when(s + AHEAD_SUM < CHUNKS)
        def _():
            add_up(s + AHEAD_SUM)

        @pl.when(k == 0)
        def _():
            now[...] = state[...]

        all_spread(s).wait_recv()
        part_rows = 64
        for g in range(NB // part_rows):
            part = slice(g * part_rows, (g + 1) * part_rows)
            inflow = own[s, part] + drive[k, part]
            for d in range(3):
                code = sums_in[s, d, part].astype(I32).astype(F32)
                code = code + (COARSE - 1.0) * (code - jnp.clip(code, -EDGE, EDGE))
                inflow = inflow + (code - MIDDLE) * dec[d, part]
            v, h, n = step_neurons(now[0, part], now[1, part], now[2, part], leak[part], inflow)
            now[0, part] = v
            now[1, part] = h
            now[2, part] = n
            volt[k, part] = v

        @pl.when(s < K)
        def _():
            ag[s + K, 0] = now[0].astype(BF)

        return carry

    lax.fori_loop(0, CHUNKS, chunk, 0)
    gate[...] = now[1:3]

    def drain(s, carry):
        all_sent(s).wait_send()
        relay_copy(s).wait_send()
        all_spread(s).wait_send()
        return carry

    lax.fori_loop(0, CHUNKS, drain, 0)


def local(
    initial_state, waveform_guess, drive_current, conductance, partners, partner_slot, cond_index, remote_block
):
    wave0 = waveform_guess.reshape(K, NB, NB)
    drive = drive_current.reshape(K, NB, NB)
    state = initial_state.reshape(3, NB, NB)
    lists = jnp.concatenate(
        [partners.T, partner_slot.T, cond_index.T, remote_block[None, :], jnp.zeros((2, NB), I32)], axis=0
    )
    dma = pltpu.SemaphoreType.DMA
    volt, gate = pl.pallas_call(
        kernel,
        out_shape=(jax.ShapeDtypeStruct((K, NB, NB), F32), jax.ShapeDtypeStruct((2, NB, NB), F32)),
        in_specs=[pl.BlockSpec(memory_space=pltpu.VMEM)] * 5,
        out_specs=(pl.BlockSpec(memory_space=pltpu.VMEM),) * 2,
        scratch_shapes=[
            pltpu.VMEM((CHUNKS, 8, NB, NB), BF),
            pltpu.VMEM((CHUNKS, NB, NB), BF),
            pltpu.VMEM((CHUNKS, 3, NB, NB), jnp.int16),
            pltpu.VMEM((CHUNKS, 3, NB, NB), jnp.int16),
            pltpu.VMEM((CHUNKS, NB, NB), F32),
            pltpu.VMEM((8, 4 * CAP, NB), BF),
            pltpu.VMEM((4, 9 * NB, NB), BF),
            pltpu.VMEM((9 * NB, NB), I32),
            pltpu.VMEM((NB, 9 * NB), BF),
            pltpu.VMEM((4 * NB, 2 * NB), BF),
            pltpu.VMEM((3, NB, NB), F32),
            pltpu.VMEM((NB, NB), F32),
            pltpu.VMEM((3, NB, NB), F32),
            pltpu.VMEM((3, NB, NB), F32),
            pltpu.VMEM((3, NB, NB), F32),
            pltpu.VMEM((4, 3, 8, NB), I32),
            pltpu.VMEM((8, 3, 8, NB), I32),
            pltpu.VMEM((8, NB), I32),
            pltpu.VMEM((8, NB), I32),
            pltpu.VMEM((3, 8, NB), F32),
            pltpu.VMEM((3, 8, NB), F32),
            dma((CHUNKS,)), dma((CHUNKS,)), dma((CHUNKS,)), dma((CHUNKS,)), dma((CHUNKS,)), dma((CHUNKS,)), dma((CHUNKS,)),
            dma((8,)), dma((8,)), dma, dma, dma((3,)), dma((3,)),
        ],
        compiler_params=pltpu.CompilerParams(
            collective_id=0, has_side_effects=True, vmem_limit_bytes=48 * 1024 * 1024
        ),
        name="relax",
    )(wave0, drive, state, conductance, lists)
    return volt.reshape(K, NB * NB), gate.reshape(2, NB * NB)


def solution(mesh):
    in_specs = (
        P(None, ("area", "dev")),
        P(None, ("area", "dev")),
        P(None, ("area", "dev")),
        P(),
        P(("area", "dev"), None),
        P(("area", "dev"), None),
        P(("area", "dev"), None),
        P(("area", "dev")),
    )
    out_specs = (P(None, ("area", "dev")), P(None, ("area", "dev")))
    return jax.shard_map(local, mesh=mesh, in_specs=in_specs, out_specs=out_specs, check_vma=False)
```

```python
import functools

import jax
import jax.numpy as jnp
from jax import lax
from jax.experimental import pallas as pl
from jax.experimental.pallas import tpu as pltpu
from jax.sharding import PartitionSpec as P

MESH = pl.DeviceIdType.MESH
K = 10
ITERS = 2
NEWTON = 3
CHUNKS = K * ITERS
NB = 128
CAP = 32
KINDS = 8
AHEAD_GATHER = 9
AHEAD_RELAY = 6
AHEAD_SUM = 4
STEPS = 2380.0
MIDDLE = 2.0 * STEPS
EDGE = 10.0 * STEPS
COARSE = 32.0
LOG2E = 1.4426950408889634
BF = jnp.bfloat16
F32 = jnp.float32
I32 = jnp.int32


def rcp(value):
    return pl.reciprocal(value, approx=True)


def gate_pair(shifted, scale):
    u = jnp.exp2(jnp.minimum(shifted * (LOG2E * scale), 20.0 * LOG2E))
    return u, 1.0 + u * u


def step_neurons(v, h, n, leak, drive_in):
    u, bottom = gate_pair(v + 5.8, 1.0 / 1.4)
    target = rcp(bottom)
    tau = 0.6 + 6.0 * (u * target)
    h = target + (h - target) * jnp.exp2((-0.05 * LOG2E) * rcp(tau))
    u, bottom = gate_pair(v + 3.0, -0.5)
    target = rcp(bottom)
    tau = 0.5 + 8.0 * (u * target)
    n = target + (n - target) * jnp.exp2((-0.05 * LOG2E) * rcp(tau))
    square = n * n
    potassium = 9.0 * (square * square)
    linear = leak + potassium + 20.1
    offset = 20.0 * v - 9.0 * potassium - 0.65 + drive_in
    sodium = 35.0 * h
    for _ in range(NEWTON):
        m = rcp(1.0 + jnp.exp2(v * (-1.25 * LOG2E) - 3.5 * 1.25 * LOG2E))
        q = sodium * (m * m * m)
        w = v - 5.5
        residual = linear * v - offset + q * w
        jacobian = linear + q * (1.0 + (3.75 * w) * (1.0 - m))
        v = v - residual * rcp(jnp.maximum(jacobian, 10.0))
    return v, h, n


def dot(a, b):
    return jnp.dot(a, b, preferred_element_type=F32)


def dot_last(a, b):
    return lax.dot_general(a, b, (((1,), (1,)), ((), ())), preferred_element_type=F32)


def kernel(
    wave_in, drive_in, state_in, cond_in, partners_in, slots_in, kinds_in, remote_in, volt_out, gate_out,
    wave0, volt_raw, gate_raw, volt, partners, slots, kinds, remotes, drive_raw, state_raw, cond, waves_f32, drive, state, ag, far, sums_out, sums_in, own, select, masks, odd, place, tables, now, leak, enc, dec, left, m1s, m1r, mys, myr, m2s, m2r,
    load, store, send1, recv1, sendr, recvr, recvy, send2, recv2, sendm1, recvm1, sendmy, recvmy, sendm2, recvm2,
):
    dev = lax.axis_index("dev")
    core, x, z = dev % 2, (dev // 2) % 4, dev // 8
    area = lax.axis_index("area")
    over_z = [((z + o) % 4) * 8 + x * 2 for o in range(4)]
    column = [(area, over_z[o] + (core + c) % 2) for c in (0, 1) for o in range(4)]
    along = [(area, z * 8 + ((x + o) % 4) * 2 + core) for o in range(4)]
    sibling = column[4]
    next_area = ((area + 1) % 4, dev)
    loads = [
        pltpu.make_async_copy(cond_in, cond, load.at[0]),
        pltpu.make_async_copy(state_in, state_raw, load.at[1]),
        pltpu.make_async_copy(drive_in, drive_raw, load.at[2]),
        pltpu.make_async_copy(wave_in, wave0, load.at[3]),
        pltpu.make_async_copy(partners_in, partners, load.at[4]),
        pltpu.make_async_copy(slots_in, slots, load.at[5]),
        pltpu.make_async_copy(kinds_in, kinds, load.at[6]),
        pltpu.make_async_copy(remote_in, remotes, load.at[7]),
    ]
    for item in loads:
        item.start()
    barrier = pltpu.get_barrier_semaphore()
    greet = column[1:] + along[1:] + [next_area, ((area + 3) % 4, dev)]
    for other in greet:
        pl.semaphore_signal(barrier, inc=1, device_id=other, device_id_type=MESH)

    for item in loads[4:]:
        item.wait()
    rows = lax.broadcasted_iota(I32, (32, NB), 0)
    target = ((z + (rows >> 3)) & 3) * 8 + ((x + rows) & 3) * 2 + ((core + (rows >> 2)) & 1)
    hit = jnp.zeros((32, NB), F32)
    slot = jnp.zeros((32, NB), I32)
    link_kind = jnp.zeros((32, NB), I32)
    for p in range(4):
        same = partners[p : p + 1, :] == target
        hit = jnp.where(same, 1.0, hit)
        slot = jnp.where(same, slots[p : p + 1, :], slot)
        link_kind = jnp.where(same, kinds[p : p + 1, :], link_kind)
    lane = lax.broadcasted_iota(I32, (NB, NB), 1)
    line = lax.broadcasted_iota(I32, (NB, NB), 0)
    rank = dot(hit.astype(BF), jnp.where(line < lane, 1.0, 0.0).astype(BF))
    rank = jnp.where(hit > 0.5, rank, -1.0).astype(I32)
    for o in range(4):
        part = slice(8 * o, 8 * o + 8)
        put = m1r.at[0] if o == 0 else m1s.at[o]
        put[0] = rank[part]
        put[1] = slot[part]
        put[2] = link_kind[part]
    m1s[0] = m1r[0]
    mys[0:1, :] = kinds[4:5, :]
    mys[1:2, :] = remotes[...]
    mys[2:8, :] = jnp.zeros((6, NB), I32)

    pl.semaphore_wait(barrier, len(greet))

    def remote(src, dst, send, recv, where):
        return pltpu.make_async_remote_copy(
            src_ref=src, dst_ref=dst, send_sem=send, recv_sem=recv,
            device_id=where, device_id_type=MESH,
        )

    def gather(s):
        mine = ag.at[s, 0]
        for o in (1, 3, 2):
            remote(mine, ag.at[s, o], send1.at[s], recv1.at[s], column[o]).start()
        remote(mine, ag.at[s, 4], send1.at[s], recvr.at[s], sibling).start()
        remote(mine, far.at[s], send1.at[s], recvy.at[s], next_area).start()

    def relay_copy(s):
        return remote(ag.at[s, pl.ds(1, 3)], ag.at[s, pl.ds(5, 3)], sendr.at[s], recvr.at[s], sibling)

    def relay(s):
        all_gathered(s).wait_recv()
        relay_copy(s).start()

    def spread(s):
        for o in (1, 3, 2):
            remote(sums_out.at[s, o - 1], sums_in.at[s, o - 1], send2.at[s], recv2.at[s], along[o]).start()

    def all_gathered(s):
        return remote(ag.at[s, pl.ds(1, 3)], ag.at[s, pl.ds(1, 3)], send1.at[s], recv1.at[s], column[1])

    def all_sent(s):
        return remote(ag.at[s, pl.ds(0, 5)], ag.at[s, pl.ds(0, 5)], send1.at[s], recv1.at[s], column[1])

    def all_relayed(s):
        return remote(ag.at[s, pl.ds(4, 4)], ag.at[s, pl.ds(4, 4)], sendr.at[s], recvr.at[s], sibling)

    def far_copy(s):
        return remote(ag.at[s, 0], far.at[s], send1.at[s], recvy.at[s], next_area)

    def all_spread(s):
        return remote(sums_out.at[s], sums_in.at[s], send2.at[s], recv2.at[s], along[1])

    def list_copy(b):
        return remote(m1s.at[b % 4], m1r.at[b], sendm1.at[b], recvm1.at[b], column[b])

    far_lists = remote(mys, myr, sendmy, recvmy, next_area)
    for b in range(1, 8):
        list_copy(b).start()
    far_lists.start()

    def split_wave(t, carry):
        column = wave0[:, pl.ds(pl.multiple_of(t * NB, NB), NB)].astype(F32)
        waves_f32[pl.ds(t, 8, stride=NB), :] = column[0:8]
        waves_f32[pl.ds(8 * NB + t, 2, stride=NB), :] = column[8:10]
        return carry

    loads[3].wait()
    lax.fori_loop(0, NB, split_wave, 0, unroll=8)
    for s in range(K):
        ag[s, 0] = waves_f32[s * NB : (s + 1) * NB, :].astype(BF)
        if s < AHEAD_GATHER:
            gather(s)
    loads[0].wait()
    for c in range(KINDS):
        tables[(c // 2) * NB : (c // 2 + 1) * NB, (c % 2) * NB : (c % 2 + 1) * NB] = cond[c]
    column_sums = [jnp.sum(cond[c].astype(F32), axis=0, keepdims=True) for c in range(KINDS)]
    column_sums = jnp.concatenate(column_sums + [jnp.zeros((NB - KINDS, NB), F32)], axis=0)
    sums_high = column_sums.astype(BF)
    column_sums = column_sums - sums_high.astype(F32)
    sums_mid = column_sums.astype(BF)
    sums_low = (column_sums - sums_mid.astype(F32)).astype(BF)

    def weigh(count):
        count = count.astype(BF)
        return dot(count, sums_high) + (dot(count, sums_mid) + dot(count, sums_low))

    for b in range(1, 8):
        list_copy(b).wait()
    far_lists.wait()

    spot = lax.broadcasted_iota(I32, (CAP, NB), 0)
    ones = jnp.ones((NB, NB), BF)
    blocks = [[] for _ in range(4)]
    of_link = [[] for _ in range(4)]
    for b in range(8):
        for d in range(4):
            row = (b // 4) * 4 + d
            chosen = m1r[b, 0, row : row + 1, :] == spot
            select[b, d * CAP : (d + 1) * CAP, :] = jnp.where(chosen, 1.0, 0.0).astype(BF)
            blocks[d].append(jnp.where(chosen, m1r[b, 1, row : row + 1, :] + 1, 0).astype(F32))
            of_link[d].append(jnp.where(chosen, m1r[b, 2, row : row + 1, :], 0).astype(F32))
    for s in range(AHEAD_RELAY - AHEAD_SUM):
        relay(s)
    links = []
    for d in range(4):
        for half in (0, 1):
            pieces = slice(4 * half, 4 * half + 4)
            links.append((
                jnp.concatenate(blocks[d][pieces], axis=0).astype(BF), jnp.concatenate(of_link[d][pieces], axis=0).astype(BF)
            ))
    links.append((
        jnp.where(line == lane, myr[1:2, :] + 1, 0).astype(F32).astype(BF),
        jnp.where(line == lane, myr[0:1, :], 0).astype(F32).astype(BF),
    ))
    eye = jnp.where(line == lane, 1.0, 0.0).astype(BF)
    counts = []
    for i, (block, table) in enumerate(links):
        part = slice(i * NB, (i + 1) * NB)
        block = dot(block, ones).astype(I32)
        table = dot(table, ones).astype(I32)
        for g in range(4):
            masks[g, part, :] = jnp.where((table >> 1) == g, 1.0, 0.0).astype(BF)
        odd[part, :] = table & 1
        to_block = dot_last(eye, jnp.where(block == lane + 1, 1.0, 0.0).astype(BF)).astype(BF)
        place[:, part] = to_block
        of_kind = jnp.where((table == lane) & (block > 0), 1.0, 0.0).astype(BF)
        counts.append(dot(to_block, of_kind))
    for d in (1, 2, 3):
        count = counts[2 * d] + counts[2 * d + 1]
        m2s[d - 1] = jnp.transpose(count)[0:8, :]
        remote(m2s.at[d - 1], m2r.at[d - 1], sendm2.at[d - 1], recvm2.at[d - 1], along[d]).start()
        bound = weigh(count)
        enc[d - 1] = jnp.where(bound > 1e-30, STEPS / bound, 0.0)
    left[...] = jnp.zeros((3, NB, NB), F32)
    leak[...] = weigh(counts[0] + counts[1]) + weigh(counts[8])

    def add_up(s):
        all_relayed(s).wait_recv()
        far_copy(s).wait_recv()
        picked = [dot(select[b], ag[s, b]).astype(BF) for b in range(8)]
        waves = [got[d * CAP : (d + 1) * CAP] for d in range(4) for got in picked]
        waves = jnp.concatenate(waves + [far[s]], axis=0)
        both = dot(jnp.concatenate([waves * masks[g] for g in range(4)], axis=1), tables[...])
        message = jnp.where(odd[...] > 0, both[:, NB:], both[:, :NB])
        high = message.astype(BF)
        message = jnp.concatenate([high, (message - high.astype(F32)).astype(BF)], axis=1)
        for d in (1, 3, 2, 0):
            part = slice(2 * d * NB, 2 * (d + 1) * NB)
            total = dot(place[:, part], message[part])
            if d == 0:
                total = total + dot(place[:, 8 * NB :], message[8 * NB :])
            total = total[:, :NB] + total[:, NB:]
            if d == 0:
                own[s] = total
            else:
                code = total * enc[d - 1] + (left[d - 1] + MIDDLE)
                inner = jnp.clip(code, -EDGE, EDGE)
                code = jnp.clip(inner + (code - inner) * (1.0 / COARSE), -32767.0, 32767.0)
                sent = jnp.round(code)
                left[d - 1] = code - sent
                sums_out[s, d - 1] = sent.astype(I32).astype(jnp.int16)
        spread(s)

    for s in range(AHEAD_SUM):
        add_up(s)
        relay(AHEAD_RELAY - AHEAD_SUM + s)

    loads[1].wait()
    loads[2].wait()

    def split_drive(t, carry):
        lanes = pl.ds(pl.multiple_of(t * NB, NB), NB)
        drive[pl.ds(t, 8, stride=NB), :] = drive_raw[0:8, lanes]
        drive[pl.ds(8 * NB + t, 2, stride=NB), :] = drive_raw[8:10, lanes]
        state[pl.ds(t, 3, stride=NB), :] = state_raw[:, lanes]
        return carry

    lax.fori_loop(0, NB, split_drive, 0, unroll=8)

    for d in (1, 2, 3):
        remote(m2s.at[d - 1], m2r.at[d - 1], sendm2.at[d - 1], recvm2.at[d - 1], along[d]).wait()
        count = jnp.transpose(jnp.concatenate([m2r[d - 1], jnp.zeros((NB - 8, NB), F32)], axis=0))
        bound = weigh(count)
        dec[d - 1] = bound * (1.0 / STEPS)
        leak[...] += bound

    def join_most(t, carry):
        volt_raw[0:8, pl.ds(pl.multiple_of(t * NB, NB), NB)] = volt[pl.ds(t, 8, stride=NB), :]
        return carry

    def join_rest(t, carry):
        lanes = pl.ds(pl.multiple_of(t * NB, NB), NB)
        volt_raw[8:10, lanes] = volt[pl.ds(8 * NB + t, 2, stride=NB), :]
        gate_raw[:, lanes] = now[pl.ds(NB + t, 2, stride=NB), :]
        return carry

    stores = [
        pltpu.make_async_copy(volt_raw.at[0:8], volt_out.at[0:8], store.at[0]),
        pltpu.make_async_copy(volt_raw.at[8:10], volt_out.at[8:10], store.at[1]),
        pltpu.make_async_copy(gate_raw, gate_out, store.at[2]),
    ]

    def chunk(s, carry):
        k = s % K

        @pl.when(s + AHEAD_GATHER < CHUNKS)
        def _():
            gather(s + AHEAD_GATHER)

        @pl.when(s + AHEAD_RELAY < CHUNKS)
        def _():
            relay(s + AHEAD_RELAY)

        @pl.when(s + AHEAD_SUM < CHUNKS)
        def _():
            add_up(s + AHEAD_SUM)

        @pl.when(k == 0)
        def _():
            now[...] = state[...]

        @pl.when(s == CHUNKS - 2)
        def _():
            lax.fori_loop(0, NB, join_most, 0, unroll=8)
            stores[0].start()

        all_spread(s).wait_recv()
        part_rows = 64
        for g in range(NB // part_rows):
            first = g * part_rows
            part = slice(first, first + part_rows)
            inflow = own[s, part] + drive[pl.ds(pl.multiple_of(k * NB + first, part_rows), part_rows), :]
            for d in range(3):
                code = sums_in[s, d, part].astype(I32).astype(F32)
                code = code + (COARSE - 1.0) * (code - jnp.clip(code, -EDGE, EDGE))
                inflow = inflow + (code - MIDDLE) * dec[d, part]
            v, h, n = (now[i * NB + first : i * NB + first + part_rows] for i in range(3))
            v, h, n = step_neurons(v, h, n, leak[part], inflow)
            now[0 * NB + first : 0 * NB + first + part_rows] = v
            now[1 * NB + first : 1 * NB + first + part_rows] = h
            now[2 * NB + first : 2 * NB + first + part_rows] = n
            volt[pl.ds(pl.multiple_of(k * NB + first, part_rows), part_rows), :] = v

        @pl.when(s < K)
        def _():
            ag[s + K, 0] = now[0:NB].astype(BF)

        return carry

    lax.fori_loop(0, CHUNKS, chunk, 0)
    lax.fori_loop(0, NB, join_rest, 0, unroll=8)
    stores[1].start()
    stores[2].start()

    def drain(s, carry):
        all_sent(s).wait_send()
        relay_copy(s).wait_send()
        all_spread(s).wait_send()
        return carry

    lax.fori_loop(0, CHUNKS, drain, 0)
    for item in stores:
        item.wait()


def local(
    initial_state, waveform_guess, drive_current, conductance, partners, partner_slot, cond_index, remote_block
):
    dma = pltpu.SemaphoreType.DMA
    volt, gate = pl.pallas_call(
        kernel,
        out_shape=(jax.ShapeDtypeStruct((K, NB * NB), F32), jax.ShapeDtypeStruct((2, NB * NB), F32)),
        in_specs=[pl.BlockSpec(memory_space=pl.ANY)] * 8,
        out_specs=(pl.BlockSpec(memory_space=pl.ANY),) * 2,
        scratch_shapes=[
            pltpu.VMEM((K, NB * NB), BF),
            pltpu.VMEM((K, NB * NB), F32),
            pltpu.VMEM((2, NB * NB), F32),
            pltpu.VMEM((K * NB, NB), F32),
            pltpu.VMEM((4, NB), I32),
            pltpu.VMEM((4, NB), I32),
            pltpu.VMEM((5, NB), I32),
            pltpu.VMEM((1, NB), I32),
            pltpu.VMEM((K, NB * NB), F32),
            pltpu.VMEM((3, NB * NB), F32),
            pltpu.VMEM((KINDS, NB, NB), BF),
            pltpu.VMEM((K * NB, NB), F32),
            pltpu.VMEM((K * NB, NB), F32),
            pltpu.VMEM((3 * NB, NB), F32),
            pltpu.VMEM((CHUNKS, 8, NB, NB), BF),
            pltpu.VMEM((CHUNKS, NB, NB), BF),
            pltpu.VMEM((CHUNKS, 3, NB, NB), jnp.int16),
            pltpu.VMEM((CHUNKS, 3, NB, NB), jnp.int16),
            pltpu.VMEM((CHUNKS, NB, NB), F32),
            pltpu.VMEM((8, 4 * CAP, NB), BF),
            pltpu.VMEM((4, 9 * NB, NB), BF),
            pltpu.VMEM((9 * NB, NB), I32),
            pltpu.VMEM((NB, 9 * NB), BF),
            pltpu.VMEM((4 * NB, 2 * NB), BF),
            pltpu.VMEM((3 * NB, NB), F32),
            pltpu.VMEM((NB, NB), F32),
            pltpu.VMEM((3, NB, NB), F32),
            pltpu.VMEM((3, NB, NB), F32),
            pltpu.VMEM((3, NB, NB), F32),
            pltpu.VMEM((4, 3, 8, NB), I32),
            pltpu.VMEM((8, 3, 8, NB), I32),
            pltpu.VMEM((8, NB), I32),
            pltpu.VMEM((8, NB), I32),
            pltpu.VMEM((3, 8, NB), F32),
            pltpu.VMEM((3, 8, NB), F32),
            dma((8,)), dma((3,)), dma((CHUNKS,)), dma((CHUNKS,)), dma((CHUNKS,)), dma((CHUNKS,)), dma((CHUNKS,)), dma((CHUNKS,)), dma((CHUNKS,)),
            dma((8,)), dma((8,)), dma, dma, dma((3,)), dma((3,)),
        ],
        compiler_params=pltpu.CompilerParams(
            collective_id=0, has_side_effects=True, vmem_limit_bytes=60 * 1024 * 1024
        ),
        name="relax",
    )(
        waveform_guess, drive_current, initial_state, conductance,
        partners.T, partner_slot.T, cond_index.T, remote_block[None, :],
    )
    return volt, gate


def solution(mesh):
    in_specs = (
        P(None, ("area", "dev")),
        P(None, ("area", "dev")),
        P(None, ("area", "dev")),
        P(),
        P(("area", "dev"), None),
        P(("area", "dev"), None),
        P(("area", "dev"), None),
        P(("area", "dev")),
    )
    out_specs = (P(None, ("area", "dev")), P(None, ("area", "dev")))
    return jax.shard_map(local, mesh=mesh, in_specs=in_specs, out_specs=out_specs, check_vma=False)
```

```python
import functools

import jax
import jax.numpy as jnp
from jax import lax
from jax.experimental import pallas as pl
from jax.experimental.pallas import tpu as pltpu
from jax.sharding import PartitionSpec as P

MESH = pl.DeviceIdType.MESH
K = 10
ITERS = 2
NEWTON = 3
CHUNKS = K * ITERS
NB = 128
CAP = 32
KINDS = 8
AHEAD_GATHER = 9
AHEAD_RELAY = 6
AHEAD_SUM = 4
STEPS = 2380.0
MIDDLE = 2.0 * STEPS
EDGE = 10.0 * STEPS
COARSE = 32.0
LOG2E = 1.4426950408889634
BF = jnp.bfloat16
F32 = jnp.float32
I32 = jnp.int32


def rcp(value):
    return pl.reciprocal(value, approx=True)


def gate_pair(shifted, scale):
    u = jnp.exp2(jnp.minimum(shifted * (LOG2E * scale), 20.0 * LOG2E))
    return u, 1.0 + u * u


def step_neurons(v, h, n, leak, drive_in):
    u, bottom = gate_pair(v + 5.8, 1.0 / 1.4)
    target = rcp(bottom)
    tau = 0.6 + 6.0 * (u * target)
    h = target + (h - target) * jnp.exp2((-0.05 * LOG2E) * rcp(tau))
    u, bottom = gate_pair(v + 3.0, -0.5)
    target = rcp(bottom)
    tau = 0.5 + 8.0 * (u * target)
    n = target + (n - target) * jnp.exp2((-0.05 * LOG2E) * rcp(tau))
    square = n * n
    potassium = 9.0 * (square * square)
    linear = leak + potassium + 20.1
    offset = 20.0 * v - 9.0 * potassium - 0.65 + drive_in
    sodium = 35.0 * h
    for _ in range(NEWTON):
        m = rcp(1.0 + jnp.exp2(v * (-1.25 * LOG2E) - 3.5 * 1.25 * LOG2E))
        q = sodium * (m * m * m)
        w = v - 5.5
        residual = linear * v - offset + q * w
        jacobian = linear + q * (1.0 + (3.75 * w) * (1.0 - m))
        v = v - residual * rcp(jnp.maximum(jacobian, 10.0))
    return v, h, n


def dot(a, b):
    return jnp.dot(a, b, preferred_element_type=F32)


def dot_last(a, b):
    return lax.dot_general(a, b, (((1,), (1,)), ((), ())), preferred_element_type=F32)


def kernel(
    wave_in, drive_in, state_in, cond_in, partners_in, slots_in, kinds_in, remote_in, volt_out, gate_out,
    wave0, volt_raw, gate_raw, volt, partners, slots, kinds, remotes, drive_raw, state_raw, cond, waves_f32, drive, state, ag, far, sums_out, sums_in, own, select, masks, odd, place, tables, now, leak, enc, dec, left, m1s, m1r, mys, myr, m2s, m2r,
    load, store, send1, recv1, sendr, recvr, recvy, send2, recv2, sendm1, recvm1, sendmy, recvmy, sendm2, recvm2,
):
    dev = lax.axis_index("dev")
    core, x, z = dev % 2, (dev // 2) % 4, dev // 8
    area = lax.axis_index("area")
    over_z = [((z + o) % 4) * 8 + x * 2 for o in range(4)]
    column = [(area, over_z[o] + (core + c) % 2) for c in (0, 1) for o in range(4)]
    along = [(area, z * 8 + ((x + o) % 4) * 2 + core) for o in range(4)]
    sibling = column[4]
    next_area = ((area + 1) % 4, dev)
    loads = [
        pltpu.make_async_copy(cond_in, cond, load.at[0]),
        pltpu.make_async_copy(state_in, state_raw, load.at[1]),
        pltpu.make_async_copy(drive_in, drive_raw, load.at[2]),
        pltpu.make_async_copy(wave_in, wave0, load.at[3]),
        pltpu.make_async_copy(partners_in, partners, load.at[4]),
        pltpu.make_async_copy(slots_in, slots, load.at[5]),
        pltpu.make_async_copy(kinds_in, kinds, load.at[6]),
        pltpu.make_async_copy(remote_in, remotes, load.at[7]),
    ]
    for item in loads:
        item.start()
    barrier = pltpu.get_barrier_semaphore()
    greet = column[1:] + along[1:] + [next_area, ((area + 3) % 4, dev)]
    for other in greet:
        pl.semaphore_signal(barrier, inc=1, device_id=other, device_id_type=MESH)

    for item in loads[4:]:
        item.wait()
    rows = lax.broadcasted_iota(I32, (32, NB), 0)
    target = ((z + (rows >> 3)) & 3) * 8 + ((x + rows) & 3) * 2 + ((core + (rows >> 2)) & 1)
    hit = jnp.zeros((32, NB), F32)
    slot = jnp.zeros((32, NB), I32)
    link_kind = jnp.zeros((32, NB), I32)
    for p in range(4):
        same = partners[p : p + 1, :] == target
        hit = jnp.where(same, 1.0, hit)
        slot = jnp.where(same, slots[p : p + 1, :], slot)
        link_kind = jnp.where(same, kinds[p : p + 1, :], link_kind)
    lane = lax.broadcasted_iota(I32, (NB, NB), 1)
    line = lax.broadcasted_iota(I32, (NB, NB), 0)
    rank = dot(hit.astype(BF), jnp.where(line < lane, 1.0, 0.0).astype(BF))
    rank = jnp.where(hit > 0.5, rank, -1.0).astype(I32)
    for o in range(4):
        part = slice(8 * o, 8 * o + 8)
        put = m1r.at[0] if o == 0 else m1s.at[o]
        put[0] = rank[part]
        put[1] = slot[part]
        put[2] = link_kind[part]
    m1s[0] = m1r[0]
    mys[0:1, :] = kinds[4:5, :]
    mys[1:2, :] = remotes[...]
    mys[2:8, :] = jnp.zeros((6, NB), I32)

    pl.semaphore_wait(barrier, len(greet))

    def remote(src, dst, send, recv, where):
        return pltpu.make_async_remote_copy(
            src_ref=src, dst_ref=dst, send_sem=send, recv_sem=recv,
            device_id=where, device_id_type=MESH,
        )

    def gather(s):
        mine = ag.at[s, 0]
        for o in (1, 3, 2):
            remote(mine, ag.at[s, o], send1.at[s], recv1.at[s], column[o]).start()
        remote(mine, ag.at[s, 4], send1.at[s], recvr.at[s], sibling).start()
        remote(mine, far.at[s], send1.at[s], recvy.at[s], next_area).start()

    def relay_copy(s):
        return remote(ag.at[s, pl.ds(1, 3)], ag.at[s, pl.ds(5, 3)], sendr.at[s], recvr.at[s], sibling)

    def relay(s):
        all_gathered(s).wait_recv()
        relay_copy(s).start()

    def spread(s):
        for o in (1, 3, 2):
            remote(sums_out.at[s, o - 1], sums_in.at[s, o - 1], send2.at[s], recv2.at[s], along[o]).start()

    def all_gathered(s):
        return remote(ag.at[s, pl.ds(1, 3)], ag.at[s, pl.ds(1, 3)], send1.at[s], recv1.at[s], column[1])

    def all_sent(s):
        return remote(ag.at[s, pl.ds(0, 5)], ag.at[s, pl.ds(0, 5)], send1.at[s], recv1.at[s], column[1])

    def all_relayed(s):
        return remote(ag.at[s, pl.ds(4, 4)], ag.at[s, pl.ds(4, 4)], sendr.at[s], recvr.at[s], sibling)

    def far_copy(s):
        return remote(ag.at[s, 0], far.at[s], send1.at[s], recvy.at[s], next_area)

    def all_spread(s):
        return remote(sums_out.at[s], sums_in.at[s], send2.at[s], recv2.at[s], along[1])

    def list_copy(b):
        return remote(m1s.at[b % 4], m1r.at[b], sendm1.at[b], recvm1.at[b], column[b])

    far_lists = remote(mys, myr, sendmy, recvmy, next_area)
    for b in range(1, 8):
        list_copy(b).start()
    far_lists.start()

    def split_wave(t, carry):
        column = wave0[:, pl.ds(pl.multiple_of(t * NB, NB), NB)].astype(F32)
        waves_f32[pl.ds(t, 8, stride=NB), :] = column[0:8]
        waves_f32[pl.ds(8 * NB + t, 2, stride=NB), :] = column[8:10]
        return carry

    loads[3].wait()
    lax.fori_loop(0, NB, split_wave, 0, unroll=8)
    for s in range(K):
        ag[s, 0] = waves_f32[s * NB : (s + 1) * NB, :].astype(BF)
        if s < AHEAD_GATHER:
            gather(s)
    loads[0].wait()
    for c in range(KINDS):
        tables[(c // 2) * NB : (c // 2 + 1) * NB, (c % 2) * NB : (c % 2 + 1) * NB] = cond[c]
    column_sums = [jnp.sum(cond[c].astype(F32), axis=0, keepdims=True) for c in range(KINDS)]
    column_sums = jnp.concatenate(column_sums + [jnp.zeros((NB - KINDS, NB), F32)], axis=0)
    sums_high = column_sums.astype(BF)
    column_sums = column_sums - sums_high.astype(F32)
    sums_mid = column_sums.astype(BF)
    sums_low = (column_sums - sums_mid.astype(F32)).astype(BF)
    sums_parts = jnp.concatenate([sums_high, sums_mid, sums_low], axis=1)

    def weigh(count):
        weighed = dot(count.astype(BF), sums_parts)
        return weighed[:, :NB] + (weighed[:, NB : 2 * NB] + weighed[:, 2 * NB :])

    for b in range(1, 8):
        list_copy(b).wait()
    far_lists.wait()

    spot = lax.broadcasted_iota(I32, (CAP, NB), 0)
    ones = jnp.ones((NB, NB), BF)
    blocks = [[] for _ in range(4)]
    of_link = [[] for _ in range(4)]
    for b in range(8):
        for d in range(4):
            row = (b // 4) * 4 + d
            chosen = m1r[b, 0, row : row + 1, :] == spot
            select[b, d * CAP : (d + 1) * CAP, :] = jnp.where(chosen, 1.0, 0.0).astype(BF)
            blocks[d].append(jnp.where(chosen, m1r[b, 1, row : row + 1, :] + 1, 0).astype(F32))
            of_link[d].append(jnp.where(chosen, m1r[b, 2, row : row + 1, :], 0).astype(F32))
    eye = jnp.where(line == lane, 1.0, 0.0)
    blocks = [block for d in range(4) for block in blocks[d]] + [eye * (myr[1:2, :] + 1).astype(F32)]
    of_link = [table for d in range(4) for table in of_link[d]] + [eye * myr[0:1, :].astype(F32)]
    block = dot(jnp.concatenate(blocks, axis=0).astype(BF), ones).astype(I32)
    table = dot(jnp.concatenate(of_link, axis=0).astype(BF), ones).astype(I32)
    lanes = lax.broadcasted_iota(I32, (9 * NB, NB), 1)
    place[...] = dot_last(eye.astype(BF), jnp.where(block == lanes + 1, 1.0, 0.0).astype(BF)).astype(BF)
    for g in range(4):
        masks[g] = jnp.where((table >> 1) == g, 1.0, 0.0).astype(BF)
    odd[...] = table & 1
    of_kind = jnp.where((table == lanes) & (block > 0), 1.0, 0.0).astype(BF)
    parts = [slice(2 * d * NB, 2 * (d + 1) * NB) for d in range(4)] + [slice(8 * NB, 9 * NB)]
    counts = [dot(place[:, part], of_kind[part]) for part in parts]
    bounds = weigh(jnp.concatenate(counts, axis=0))
    for d in (1, 2, 3):
        bound = bounds[d * NB : (d + 1) * NB]
        enc[d - 1] = jnp.where(bound > 1e-30, STEPS / bound, 0.0)
    for s in range(AHEAD_RELAY - AHEAD_SUM):
        relay(s)
    for d in (1, 2, 3):
        m2s[d - 1] = jnp.transpose(counts[d])[0:8, :]
        remote(m2s.at[d - 1], m2r.at[d - 1], sendm2.at[d - 1], recvm2.at[d - 1], along[d]).start()
    left[...] = jnp.zeros((3, NB, NB), F32)
    leak[...] = bounds[0:NB] + bounds[4 * NB :]

    def add_up(s):
        all_relayed(s).wait_recv()
        far_copy(s).wait_recv()
        picked = [dot(select[b], ag[s, b]).astype(BF) for b in range(8)]
        waves = [got[d * CAP : (d + 1) * CAP] for d in range(4) for got in picked]
        waves = jnp.concatenate(waves + [far[s]], axis=0)
        both = dot(jnp.concatenate([waves * masks[g] for g in range(4)], axis=1), tables[...])
        message = jnp.where(odd[...] > 0, both[:, NB:], both[:, :NB])
        high = message.astype(BF)
        message = jnp.concatenate([high, (message - high.astype(F32)).astype(BF)], axis=1)
        for d in (1, 3, 2, 0):
            part = slice(2 * d * NB, 2 * (d + 1) * NB)
            total = dot(place[:, part], message[part])
            if d == 0:
                total = total + dot(place[:, 8 * NB :], message[8 * NB :])
            total = total[:, :NB] + total[:, NB:]
            if d == 0:
                own[s] = total
            else:
                code = total * enc[d - 1] + (left[d - 1] + MIDDLE)
                inner = jnp.clip(code, -EDGE, EDGE)
                code = jnp.clip(inner + (code - inner) * (1.0 / COARSE), -32767.0, 32767.0)
                sent = jnp.round(code)
                left[d - 1] = code - sent
                sums_out[s, d - 1] = sent.astype(I32).astype(jnp.int16)
        spread(s)

    for s in range(AHEAD_SUM):
        add_up(s)
        relay(AHEAD_RELAY - AHEAD_SUM + s)

    loads[1].wait()
    loads[2].wait()

    def split_drive(t, carry):
        lanes = pl.ds(pl.multiple_of(t * NB, NB), NB)
        drive[pl.ds(t, 8, stride=NB), :] = drive_raw[0:8, lanes]
        drive[pl.ds(8 * NB + t, 2, stride=NB), :] = drive_raw[8:10, lanes]
        state[pl.ds(t, 3, stride=NB), :] = state_raw[:, lanes]
        return carry

    lax.fori_loop(0, NB, split_drive, 0, unroll=8)

    for d in (1, 2, 3):
        remote(m2s.at[d - 1], m2r.at[d - 1], sendm2.at[d - 1], recvm2.at[d - 1], along[d]).wait()
    rest = jnp.zeros((NB - 8, NB), F32)
    counts = [jnp.transpose(jnp.concatenate([m2r[d], rest], axis=0)) for d in range(3)]
    bounds = weigh(jnp.concatenate(counts, axis=0))
    for d in range(3):
        bound = bounds[d * NB : (d + 1) * NB]
        dec[d] = bound * (1.0 / STEPS)
        leak[...] += bound

    def join_most(t, carry):
        volt_raw[0:8, pl.ds(pl.multiple_of(t * NB, NB), NB)] = volt[pl.ds(t, 8, stride=NB), :]
        return carry

    def join_rest(t, carry):
        lanes = pl.ds(pl.multiple_of(t * NB, NB), NB)
        volt_raw[8:10, lanes] = volt[pl.ds(8 * NB + t, 2, stride=NB), :]
        gate_raw[:, lanes] = now[pl.ds(NB + t, 2, stride=NB), :]
        return carry

    stores = [
        pltpu.make_async_copy(volt_raw.at[0:8], volt_out.at[0:8], store.at[0]),
        pltpu.make_async_copy(volt_raw.at[8:10], volt_out.at[8:10], store.at[1]),
        pltpu.make_async_copy(gate_raw, gate_out, store.at[2]),
    ]

    def chunk(s, carry):
        k = s % K

        @pl.when(s + AHEAD_GATHER < CHUNKS)
        def _():
            gather(s + AHEAD_GATHER)

        @pl.when(s + AHEAD_RELAY < CHUNKS)
        def _():
            relay(s + AHEAD_RELAY)

        @pl.when(s + AHEAD_SUM < CHUNKS)
        def _():
            add_up(s + AHEAD_SUM)

        @pl.when(k == 0)
        def _():
            now[...] = state[...]

        @pl.when(s == CHUNKS - 2)
        def _():
            lax.fori_loop(0, NB, join_most, 0, unroll=8)
            stores[0].start()

        all_spread(s).wait_recv()
        part_rows = 64
        for g in range(NB // part_rows):
            first = g * part_rows
            part = slice(first, first + part_rows)
            inflow = own[s, part] + drive[pl.ds(pl.multiple_of(k * NB + first, part_rows), part_rows), :]
            for d in range(3):
                code = sums_in[s, d, part].astype(I32).astype(F32)
                code = code + (COARSE - 1.0) * (code - jnp.clip(code, -EDGE, EDGE))
                inflow = inflow + (code - MIDDLE) * dec[d, part]
            v, h, n = (now[i * NB + first : i * NB + first + part_rows] for i in range(3))
            v, h, n = step_neurons(v, h, n, leak[part], inflow)
            now[0 * NB + first : 0 * NB + first + part_rows] = v
            now[1 * NB + first : 1 * NB + first + part_rows] = h
            now[2 * NB + first : 2 * NB + first + part_rows] = n
            volt[pl.ds(pl.multiple_of(k * NB + first, part_rows), part_rows), :] = v

        @pl.when(s < K)
        def _():
            ag[s + K, 0] = now[0:NB].astype(BF)

        return carry

    lax.fori_loop(0, CHUNKS, chunk, 0)
    lax.fori_loop(0, NB, join_rest, 0, unroll=8)
    stores[1].start()
    stores[2].start()

    def drain(s, carry):
        all_sent(s).wait_send()
        relay_copy(s).wait_send()
        all_spread(s).wait_send()
        return carry

    lax.fori_loop(0, CHUNKS, drain, 0)
    for item in stores:
        item.wait()


def local(
    initial_state, waveform_guess, drive_current, conductance, partners, partner_slot, cond_index, remote_block
):
    dma = pltpu.SemaphoreType.DMA
    volt, gate = pl.pallas_call(
        kernel,
        out_shape=(jax.ShapeDtypeStruct((K, NB * NB), F32), jax.ShapeDtypeStruct((2, NB * NB), F32)),
        in_specs=[pl.BlockSpec(memory_space=pl.ANY)] * 8,
        out_specs=(pl.BlockSpec(memory_space=pl.ANY),) * 2,
        scratch_shapes=[
            pltpu.VMEM((K, NB * NB), BF),
            pltpu.VMEM((K, NB * NB), F32),
            pltpu.VMEM((2, NB * NB), F32),
            pltpu.VMEM((K * NB, NB), F32),
            pltpu.VMEM((4, NB), I32),
            pltpu.VMEM((4, NB), I32),
            pltpu.VMEM((5, NB), I32),
            pltpu.VMEM((1, NB), I32),
            pltpu.VMEM((K, NB * NB), F32),
            pltpu.VMEM((3, NB * NB), F32),
            pltpu.VMEM((KINDS, NB, NB), BF),
            pltpu.VMEM((K * NB, NB), F32),
            pltpu.VMEM((K * NB, NB), F32),
            pltpu.VMEM((3 * NB, NB), F32),
            pltpu.VMEM((CHUNKS, 8, NB, NB), BF),
            pltpu.VMEM((CHUNKS, NB, NB), BF),
            pltpu.VMEM((CHUNKS, 3, NB, NB), jnp.int16),
            pltpu.VMEM((CHUNKS, 3, NB, NB), jnp.int16),
            pltpu.VMEM((CHUNKS, NB, NB), F32),
            pltpu.VMEM((8, 4 * CAP, NB), BF),
            pltpu.VMEM((4, 9 * NB, NB), BF),
            pltpu.VMEM((9 * NB, NB), I32),
            pltpu.VMEM((NB, 9 * NB), BF),
            pltpu.VMEM((4 * NB, 2 * NB), BF),
            pltpu.VMEM((3 * NB, NB), F32),
            pltpu.VMEM((NB, NB), F32),
            pltpu.VMEM((3, NB, NB), F32),
            pltpu.VMEM((3, NB, NB), F32),
            pltpu.VMEM((3, NB, NB), F32),
            pltpu.VMEM((4, 3, 8, NB), I32),
            pltpu.VMEM((8, 3, 8, NB), I32),
            pltpu.VMEM((8, NB), I32),
            pltpu.VMEM((8, NB), I32),
            pltpu.VMEM((3, 8, NB), F32),
            pltpu.VMEM((3, 8, NB), F32),
            dma((8,)), dma((3,)), dma((CHUNKS,)), dma((CHUNKS,)), dma((CHUNKS,)), dma((CHUNKS,)), dma((CHUNKS,)), dma((CHUNKS,)), dma((CHUNKS,)),
            dma((8,)), dma((8,)), dma, dma, dma((3,)), dma((3,)),
        ],
        compiler_params=pltpu.CompilerParams(
            collective_id=0, has_side_effects=True, vmem_limit_bytes=60 * 1024 * 1024
        ),
        name="relax",
    )(
        waveform_guess, drive_current, initial_state, conductance,
        partners.T, partner_slot.T, cond_index.T, remote_block[None, :],
    )

    def hand_on(volt_in, gate_in, volt_out, gate_out, volt_held, gate_held, taken, done):
        parts = 4
        size = NB * NB // parts
        hops = [(gate_in, gate_held, gate_out)]
        for i in range(parts):
            lanes = pl.ds(i * size, size)
            hops.append((volt_in.at[:, lanes], volt_held.at[:, lanes], volt_out.at[:, lanes]))
        loads = [pltpu.make_async_copy(a, b, taken.at[i]) for i, (a, b, c) in enumerate(hops)]
        stores = [pltpu.make_async_copy(b, c, done.at[i]) for i, (a, b, c) in enumerate(hops)]
        for item in loads:
            item.start()
        for i in range(parts + 1):
            loads[i].wait()
            stores[i].start()
        for item in stores:
            item.wait()

    return pl.pallas_call(
        hand_on,
        out_shape=(jax.ShapeDtypeStruct(volt.shape, F32), jax.ShapeDtypeStruct(gate.shape, F32)),
        in_specs=[pl.BlockSpec(memory_space=pl.ANY)] * 2,
        out_specs=(pl.BlockSpec(memory_space=pl.ANY),) * 2,
        scratch_shapes=[pltpu.VMEM(volt.shape, F32), pltpu.VMEM(gate.shape, F32), dma((5,)), dma((5,))],
        name="hand_on",
    )(volt, gate)


def solution(mesh):
    in_specs = (
        P(None, ("area", "dev")),
        P(None, ("area", "dev")),
        P(None, ("area", "dev")),
        P(),
        P(("area", "dev"), None),
        P(("area", "dev"), None),
        P(("area", "dev"), None),
        P(("area", "dev")),
    )
    out_specs = (P(None, ("area", "dev")), P(None, ("area", "dev")))
    return jax.shard_map(local, mesh=mesh, in_specs=in_specs, out_specs=out_specs, check_vma=False)
```

```python
import functools

import jax
import jax.numpy as jnp
from jax import lax
from jax.experimental import pallas as pl
from jax.experimental.pallas import tpu as pltpu
from jax.sharding import PartitionSpec as P

MESH = pl.DeviceIdType.MESH
K = 10
ITERS = 2
NEWTON = 3
CHUNKS = K * ITERS
NB = 128
CAP = 32
KINDS = 8
AHEAD_GATHER = 9
AHEAD_RELAY = 6
AHEAD_SUM = 4
STEPS = 2380.0
MIDDLE = 2.0 * STEPS
EDGE = 10.0 * STEPS
COARSE = 32.0
LOG2E = 1.4426950408889634
BF = jnp.bfloat16
F32 = jnp.float32
I32 = jnp.int32


def rcp(value):
    return pl.reciprocal(value, approx=True)


def gate_pair(shifted, scale):
    u = jnp.exp2(jnp.minimum(shifted * (LOG2E * scale), 20.0 * LOG2E))
    return u, 1.0 + u * u


def step_neurons(v, h, n, leak, drive_in):
    u, bottom = gate_pair(v + 5.8, 1.0 / 1.4)
    target = rcp(bottom)
    tau = 0.6 + 6.0 * (u * target)
    h = target + (h - target) * jnp.exp2((-0.05 * LOG2E) * rcp(tau))
    u, bottom = gate_pair(v + 3.0, -0.5)
    target = rcp(bottom)
    tau = 0.5 + 8.0 * (u * target)
    n = target + (n - target) * jnp.exp2((-0.05 * LOG2E) * rcp(tau))
    square = n * n
    potassium = 9.0 * (square * square)
    linear = leak + potassium + 20.1
    offset = 20.0 * v - 9.0 * potassium - 0.65 + drive_in
    sodium = 35.0 * h
    for _ in range(NEWTON):
        m = rcp(1.0 + jnp.exp2(v * (-1.25 * LOG2E) - 3.5 * 1.25 * LOG2E))
        q = sodium * (m * m * m)
        w = v - 5.5
        residual = linear * v - offset + q * w
        jacobian = linear + q * (1.0 + (3.75 * w) * (1.0 - m))
        v = v - residual * rcp(jnp.maximum(jacobian, 10.0))
    return v, h, n


def dot(a, b):
    return jnp.dot(a, b, preferred_element_type=F32)


def dot_last(a, b):
    return lax.dot_general(a, b, (((1,), (1,)), ((), ())), preferred_element_type=F32)


def kernel(
    wave_in, drive_in, state_in, cond_in, partners_in, slots_in, kinds_in, remote_in, volt_out, gate_out,
    wave0, volt_raw, gate_raw, volt, partners, slots, kinds, remotes, drive_raw, state_raw, cond, waves_f32, drive, state, ag, far, sums_out, sums_in, own, select, masks, odd, place, tables, now, leak, enc, dec, left, m1s, m1r, mys, myr, m2s, m2r,
    load, store, send1, recv1, sendr, recvr, recvy, send2, recv2, sendm1, recvm1, sendmy, recvmy, sendm2, recvm2,
):
    dev = lax.axis_index("dev")
    core, x, z = dev % 2, (dev // 2) % 4, dev // 8
    area = lax.axis_index("area")
    over_z = [((z + o) % 4) * 8 + x * 2 for o in range(4)]
    column = [(area, over_z[o] + (core + c) % 2) for c in (0, 1) for o in range(4)]
    along = [(area, z * 8 + ((x + o) % 4) * 2 + core) for o in range(4)]
    sibling = column[4]
    next_area = ((area + 1) % 4, dev)
    barrier = pltpu.get_barrier_semaphore()
    greet = column[1:] + along[1:] + [next_area, ((area + 3) % 4, dev)]
    for other in greet:
        pl.semaphore_signal(barrier, inc=1, device_id=other, device_id_type=MESH)

    loads = [
        pltpu.make_async_copy(cond_in, cond, load.at[0]),
        pltpu.make_async_copy(state_in, state_raw, load.at[1]),
        pltpu.make_async_copy(drive_in, drive_raw, load.at[2]),
        pltpu.make_async_copy(wave_in, wave0, load.at[3]),
        pltpu.make_async_copy(partners_in, partners, load.at[4]),
        pltpu.make_async_copy(slots_in, slots, load.at[5]),
        pltpu.make_async_copy(kinds_in, kinds, load.at[6]),
        pltpu.make_async_copy(remote_in, remotes, load.at[7]),
    ]
    for item in loads[4:] + [loads[3], loads[0], loads[1], loads[2]]:
        item.start()
    for item in loads[4:]:
        item.wait()
    rows = lax.broadcasted_iota(I32, (32, NB), 0)
    target = ((z + (rows >> 3)) & 3) * 8 + ((x + rows) & 3) * 2 + ((core + (rows >> 2)) & 1)
    hit = jnp.zeros((32, NB), F32)
    slot = jnp.zeros((32, NB), I32)
    link_kind = jnp.zeros((32, NB), I32)
    for p in range(4):
        same = partners[p : p + 1, :] == target
        hit = jnp.where(same, 1.0, hit)
        slot = jnp.where(same, slots[p : p + 1, :], slot)
        link_kind = jnp.where(same, kinds[p : p + 1, :], link_kind)
    lane = lax.broadcasted_iota(I32, (NB, NB), 1)
    line = lax.broadcasted_iota(I32, (NB, NB), 0)
    rank = dot(hit.astype(BF), jnp.where(line < lane, 1.0, 0.0).astype(BF))
    rank = jnp.where(hit > 0.5, rank, -1.0).astype(I32)
    for o in range(4):
        part = slice(8 * o, 8 * o + 8)
        put = m1r.at[0] if o == 0 else m1s.at[o]
        put[0] = rank[part]
        put[1] = slot[part]
        put[2] = link_kind[part]
    m1s[0] = m1r[0]
    mys[0:1, :] = kinds[4:5, :]
    mys[1:2, :] = remotes[...]
    mys[2:8, :] = jnp.zeros((6, NB), I32)

    pl.semaphore_wait(barrier, len(greet))

    def remote(src, dst, send, recv, where):
        return pltpu.make_async_remote_copy(
            src_ref=src, dst_ref=dst, send_sem=send, recv_sem=recv,
            device_id=where, device_id_type=MESH,
        )

    def gather(s):
        mine = ag.at[s, 0]
        for o in (1, 3, 2):
            remote(mine, ag.at[s, o], send1.at[s], recv1.at[s], column[o]).start()
        remote(mine, ag.at[s, 4], send1.at[s], recvr.at[s], sibling).start()
        remote(mine, far.at[s], send1.at[s], recvy.at[s], next_area).start()

    def relay_copy(s):
        return remote(ag.at[s, pl.ds(1, 3)], ag.at[s, pl.ds(5, 3)], sendr.at[s], recvr.at[s], sibling)

    def relay(s):
        all_gathered(s).wait_recv()
        relay_copy(s).start()

    def spread(s):
        for o in (1, 3, 2):
            remote(sums_out.at[s, o - 1], sums_in.at[s, o - 1], send2.at[s], recv2.at[s], along[o]).start()

    def all_gathered(s):
        return remote(ag.at[s, pl.ds(1, 3)], ag.at[s, pl.ds(1, 3)], send1.at[s], recv1.at[s], column[1])

    def all_sent(s):
        return remote(ag.at[s, pl.ds(0, 5)], ag.at[s, pl.ds(0, 5)], send1.at[s], recv1.at[s], column[1])

    def all_relayed(s):
        return remote(ag.at[s, pl.ds(4, 4)], ag.at[s, pl.ds(4, 4)], sendr.at[s], recvr.at[s], sibling)

    def far_copy(s):
        return remote(ag.at[s, 0], far.at[s], send1.at[s], recvy.at[s], next_area)

    def all_spread(s):
        return remote(sums_out.at[s], sums_in.at[s], send2.at[s], recv2.at[s], along[1])

    def list_copy(b):
        return remote(m1s.at[b % 4], m1r.at[b], sendm1.at[b], recvm1.at[b], column[b])

    far_lists = remote(mys, myr, sendmy, recvmy, next_area)
    for b in range(1, 8):
        list_copy(b).start()
    far_lists.start()

    def split_wave(t, carry):
        column = wave0[:, pl.ds(pl.multiple_of(t * NB, NB), NB)].astype(F32)
        waves_f32[pl.ds(t, 8, stride=NB), :] = column[0:8]
        waves_f32[pl.ds(8 * NB + t, 2, stride=NB), :] = column[8:10]
        return carry

    loads[3].wait()
    lax.fori_loop(0, NB, split_wave, 0, unroll=8)
    for s in range(K):
        ag[s, 0] = waves_f32[s * NB : (s + 1) * NB, :].astype(BF)
        if s < AHEAD_GATHER:
            gather(s)
    loads[0].wait()
    for c in range(KINDS):
        tables[(c // 2) * NB : (c // 2 + 1) * NB, (c % 2) * NB : (c % 2 + 1) * NB] = cond[c]
    column_sums = [jnp.sum(cond[c].astype(F32), axis=0, keepdims=True) for c in range(KINDS)]
    column_sums = jnp.concatenate(column_sums + [jnp.zeros((NB - KINDS, NB), F32)], axis=0)
    sums_high = column_sums.astype(BF)
    column_sums = column_sums - sums_high.astype(F32)
    sums_mid = column_sums.astype(BF)
    sums_low = (column_sums - sums_mid.astype(F32)).astype(BF)
    sums_parts = jnp.concatenate([sums_high, sums_mid, sums_low], axis=1)

    def weigh(count):
        weighed = dot(count.astype(BF), sums_parts)
        return weighed[:, :NB] + (weighed[:, NB : 2 * NB] + weighed[:, 2 * NB :])

    for b in range(1, 8):
        list_copy(b).wait()
    far_lists.wait()

    spot = lax.broadcasted_iota(I32, (CAP, NB), 0)
    ones = jnp.ones((NB, NB), BF)
    blocks = [[] for _ in range(4)]
    of_link = [[] for _ in range(4)]
    for b in range(8):
        for d in range(4):
            row = (b // 4) * 4 + d
            chosen = m1r[b, 0, row : row + 1, :] == spot
            select[b, d * CAP : (d + 1) * CAP, :] = jnp.where(chosen, 1.0, 0.0).astype(BF)
            blocks[d].append(jnp.where(chosen, m1r[b, 1, row : row + 1, :] + 1, 0).astype(F32))
            of_link[d].append(jnp.where(chosen, m1r[b, 2, row : row + 1, :], 0).astype(F32))
    eye = jnp.where(line == lane, 1.0, 0.0)
    blocks = [block for d in range(4) for block in blocks[d]] + [eye * (myr[1:2, :] + 1).astype(F32)]
    of_link = [table for d in range(4) for table in of_link[d]] + [eye * myr[0:1, :].astype(F32)]
    block = dot(jnp.concatenate(blocks, axis=0).astype(BF), ones).astype(I32)
    table = dot(jnp.concatenate(of_link, axis=0).astype(BF), ones).astype(I32)
    lanes = lax.broadcasted_iota(I32, (9 * NB, NB), 1)
    place[...] = dot_last(eye.astype(BF), jnp.where(block == lanes + 1, 1.0, 0.0).astype(BF)).astype(BF)
    for g in range(4):
        masks[g] = jnp.where((table >> 1) == g, 1.0, 0.0).astype(BF)
    odd[...] = table & 1
    of_kind = jnp.where((table == lanes) & (block > 0), 1.0, 0.0).astype(BF)
    parts = [slice(2 * d * NB, 2 * (d + 1) * NB) for d in range(4)] + [slice(8 * NB, 9 * NB)]
    counts = [dot(place[:, part], of_kind[part]) for part in parts]
    bounds = weigh(jnp.concatenate(counts, axis=0))
    for d in (1, 2, 3):
        bound = bounds[d * NB : (d + 1) * NB]
        enc[d - 1] = jnp.where(bound > 1e-30, STEPS / bound, 0.0)
    for s in range(AHEAD_RELAY - AHEAD_SUM):
        relay(s)
    for d in (1, 2, 3):
        m2s[d - 1] = jnp.transpose(counts[d])[0:8, :]
        remote(m2s.at[d - 1], m2r.at[d - 1], sendm2.at[d - 1], recvm2.at[d - 1], along[d]).start()
    left[...] = jnp.zeros((3, NB, NB), F32)
    leak[...] = bounds[0:NB] + bounds[4 * NB :]

    def add_up(s):
        all_relayed(s).wait_recv()
        far_copy(s).wait_recv()
        picked = [dot(select[b], ag[s, b]).astype(BF) for b in range(8)]
        waves = [got[d * CAP : (d + 1) * CAP] for d in range(4) for got in picked]
        waves = jnp.concatenate(waves + [far[s]], axis=0)
        both = dot(jnp.concatenate([waves * masks[g] for g in range(4)], axis=1), tables[...])
        message = jnp.where(odd[...] > 0, both[:, NB:], both[:, :NB])
        high = message.astype(BF)
        message = jnp.concatenate([high, (message - high.astype(F32)).astype(BF)], axis=1)
        for d in (1, 3, 2, 0):
            part = slice(2 * d * NB, 2 * (d + 1) * NB)
            total = dot(place[:, part], message[part])
            if d == 0:
                total = total + dot(place[:, 8 * NB :], message[8 * NB :])
            total = total[:, :NB] + total[:, NB:]
            if d == 0:
                own[s] = total
            else:
                code = total * enc[d - 1] + (left[d - 1] + MIDDLE)
                inner = jnp.clip(code, -EDGE, EDGE)
                code = jnp.clip(inner + (code - inner) * (1.0 / COARSE), -32767.0, 32767.0)
                sent = jnp.round(code)
                left[d - 1] = code - sent
                sums_out[s, d - 1] = sent.astype(I32).astype(jnp.int16)
        spread(s)

    for s in range(AHEAD_SUM):
        add_up(s)
        relay(AHEAD_RELAY - AHEAD_SUM + s)

    loads[1].wait()
    loads[2].wait()

    def split_drive(t, carry):
        lanes = pl.ds(pl.multiple_of(t * NB, NB), NB)
        drive[pl.ds(t, 8, stride=NB), :] = drive_raw[0:8, lanes]
        drive[pl.ds(8 * NB + t, 2, stride=NB), :] = drive_raw[8:10, lanes]
        state[pl.ds(t, 3, stride=NB), :] = state_raw[:, lanes]
        return carry

    lax.fori_loop(0, NB, split_drive, 0, unroll=8)

    for d in (1, 2, 3):
        remote(m2s.at[d - 1], m2r.at[d - 1], sendm2.at[d - 1], recvm2.at[d - 1], along[d]).wait()
    rest = jnp.zeros((NB - 8, NB), F32)
    counts = [jnp.transpose(jnp.concatenate([m2r[d], rest], axis=0)) for d in range(3)]
    bounds = weigh(jnp.concatenate(counts, axis=0))
    for d in range(3):
        bound = bounds[d * NB : (d + 1) * NB]
        dec[d] = bound * (1.0 / STEPS)
        leak[...] += bound

    def join_most(t, carry):
        volt_raw[0:8, pl.ds(pl.multiple_of(t * NB, NB), NB)] = volt[pl.ds(t, 8, stride=NB), :]
        return carry

    def join_rest(t, carry):
        lanes = pl.ds(pl.multiple_of(t * NB, NB), NB)
        volt_raw[8:10, lanes] = volt[pl.ds(8 * NB + t, 2, stride=NB), :]
        gate_raw[:, lanes] = now[pl.ds(NB + t, 2, stride=NB), :]
        return carry

    stores = [
        pltpu.make_async_copy(volt_raw.at[0:8], volt_out.at[0:8], store.at[0]),
        pltpu.make_async_copy(volt_raw.at[8:10], volt_out.at[8:10], store.at[1]),
        pltpu.make_async_copy(gate_raw, gate_out, store.at[2]),
    ]

    def chunk(s, carry):
        k = s % K

        @pl.when(s + AHEAD_GATHER < CHUNKS)
        def _():
            gather(s + AHEAD_GATHER)

        @pl.when(s + AHEAD_SUM < CHUNKS)
        def _():
            add_up(s + AHEAD_SUM)

        @pl.when(s + AHEAD_RELAY < CHUNKS)
        def _():
            relay(s + AHEAD_RELAY)

        @pl.when(k == 0)
        def _():
            now[...] = state[...]

        @pl.when(s == CHUNKS - 2)
        def _():
            lax.fori_loop(0, NB, join_most, 0, unroll=8)
            stores[0].start()

        all_spread(s).wait_recv()
        part_rows = 64
        for g in range(NB // part_rows):
            first = g * part_rows
            part = slice(first, first + part_rows)
            inflow = own[s, part] + drive[pl.ds(pl.multiple_of(k * NB + first, part_rows), part_rows), :]
            for d in range(3):
                code = sums_in[s, d, part].astype(I32).astype(F32)
                code = code + (COARSE - 1.0) * (code - jnp.clip(code, -EDGE, EDGE))
                inflow = inflow + (code - MIDDLE) * dec[d, part]
            v, h, n = (now[i * NB + first : i * NB + first + part_rows] for i in range(3))
            v, h, n = step_neurons(v, h, n, leak[part], inflow)
            now[0 * NB + first : 0 * NB + first + part_rows] = v
            now[1 * NB + first : 1 * NB + first + part_rows] = h
            now[2 * NB + first : 2 * NB + first + part_rows] = n
            volt[pl.ds(pl.multiple_of(k * NB + first, part_rows), part_rows), :] = v

        @pl.when(s < K)
        def _():
            ag[s + K, 0] = now[0:NB].astype(BF)

        return carry

    lax.fori_loop(0, CHUNKS, chunk, 0)
    lax.fori_loop(0, NB, join_rest, 0, unroll=8)
    stores[1].start()
    stores[2].start()

    def drain(s, carry):
        all_sent(s).wait_send()
        relay_copy(s).wait_send()
        all_spread(s).wait_send()
        return carry

    lax.fori_loop(0, CHUNKS, drain, 0)
    for item in stores:
        item.wait()


def local(
    initial_state, waveform_guess, drive_current, conductance, partners, partner_slot, cond_index, remote_block
):
    dma = pltpu.SemaphoreType.DMA
    volt, gate = pl.pallas_call(
        kernel,
        out_shape=(jax.ShapeDtypeStruct((K, NB * NB), F32), jax.ShapeDtypeStruct((2, NB * NB), F32)),
        in_specs=[pl.BlockSpec(memory_space=pl.ANY)] * 8,
        out_specs=(pl.BlockSpec(memory_space=pl.ANY),) * 2,
        scratch_shapes=[
            pltpu.VMEM((K, NB * NB), BF),
            pltpu.VMEM((K, NB * NB), F32),
            pltpu.VMEM((2, NB * NB), F32),
            pltpu.VMEM((K * NB, NB), F32),
            pltpu.VMEM((4, NB), I32),
            pltpu.VMEM((4, NB), I32),
            pltpu.VMEM((5, NB), I32),
            pltpu.VMEM((1, NB), I32),
            pltpu.VMEM((K, NB * NB), F32),
            pltpu.VMEM((3, NB * NB), F32),
            pltpu.VMEM((KINDS, NB, NB), BF),
            pltpu.VMEM((K * NB, NB), F32),
            pltpu.VMEM((K * NB, NB), F32),
            pltpu.VMEM((3 * NB, NB), F32),
            pltpu.VMEM((CHUNKS, 8, NB, NB), BF),
            pltpu.VMEM((CHUNKS, NB, NB), BF),
            pltpu.VMEM((CHUNKS, 3, NB, NB), jnp.int16),
            pltpu.VMEM((CHUNKS, 3, NB, NB), jnp.int16),
            pltpu.VMEM((CHUNKS, NB, NB), F32),
            pltpu.VMEM((8, 4 * CAP, NB), BF),
            pltpu.VMEM((4, 9 * NB, NB), BF),
            pltpu.VMEM((9 * NB, NB), I32),
            pltpu.VMEM((NB, 9 * NB), BF),
            pltpu.VMEM((4 * NB, 2 * NB), BF),
            pltpu.VMEM((3 * NB, NB), F32),
            pltpu.VMEM((NB, NB), F32),
            pltpu.VMEM((3, NB, NB), F32),
            pltpu.VMEM((3, NB, NB), F32),
            pltpu.VMEM((3, NB, NB), F32),
            pltpu.VMEM((4, 3, 8, NB), I32),
            pltpu.VMEM((8, 3, 8, NB), I32),
            pltpu.VMEM((8, NB), I32),
            pltpu.VMEM((8, NB), I32),
            pltpu.VMEM((3, 8, NB), F32),
            pltpu.VMEM((3, 8, NB), F32),
            dma((8,)), dma((3,)), dma((CHUNKS,)), dma((CHUNKS,)), dma((CHUNKS,)), dma((CHUNKS,)), dma((CHUNKS,)), dma((CHUNKS,)), dma((CHUNKS,)),
            dma((8,)), dma((8,)), dma, dma, dma((3,)), dma((3,)),
        ],
        compiler_params=pltpu.CompilerParams(
            collective_id=0, has_side_effects=True, vmem_limit_bytes=60 * 1024 * 1024
        ),
        name="relax",
    )(
        waveform_guess, drive_current, initial_state, conductance,
        partners.T, partner_slot.T, cond_index.T, remote_block[None, :],
    )

    def hand_on(volt_in, gate_in, volt_out, gate_out, volt_held, gate_held, taken, done):
        parts = 4
        size = NB * NB // parts
        hops = [(gate_in, gate_held, gate_out)]
        for i in range(parts):
            lanes = pl.ds(i * size, size)
            hops.append((volt_in.at[:, lanes], volt_held.at[:, lanes], volt_out.at[:, lanes]))
        loads = [pltpu.make_async_copy(a, b, taken.at[i]) for i, (a, b, c) in enumerate(hops)]
        stores = [pltpu.make_async_copy(b, c, done.at[i]) for i, (a, b, c) in enumerate(hops)]
        for item in loads:
            item.start()
        for i in range(parts + 1):
            loads[i].wait()
            stores[i].start()
        for item in stores:
            item.wait()

    return pl.pallas_call(
        hand_on,
        out_shape=(jax.ShapeDtypeStruct(volt.shape, F32), jax.ShapeDtypeStruct(gate.shape, F32)),
        in_specs=[pl.BlockSpec(memory_space=pl.ANY)] * 2,
        out_specs=(pl.BlockSpec(memory_space=pl.ANY),) * 2,
        scratch_shapes=[pltpu.VMEM(volt.shape, F32), pltpu.VMEM(gate.shape, F32), dma((5,)), dma((5,))],
        name="hand_on",
    )(volt, gate)


def solution(mesh):
    in_specs = (
        P(None, ("area", "dev")),
        P(None, ("area", "dev")),
        P(None, ("area", "dev")),
        P(),
        P(("area", "dev"), None),
        P(("area", "dev"), None),
        P(("area", "dev"), None),
        P(("area", "dev")),
    )
    out_specs = (P(None, ("area", "dev")), P(None, ("area", "dev")))
    return jax.shard_map(local, mesh=mesh, in_specs=in_specs, out_specs=out_specs, check_vma=False)
```
